256 devices in a mesh: tm: 32 (over z_lo, x, core), tp: 8 (over y, z_hi).
Axes of the slice: x: 4, y: 4, z: 8 (z_hi: 2, z_lo: 4; z = z_hi * 4 + z_lo), core: 2. Of those that a mesh axis runs over, the one named last changes fastest.
Arguments:
- trajectory: float32 [64, 128, 64], P('tm', 'tp'), may hold values from -6 to 6
- window_start: int32 [1], replicated, may hold values from 0 to 48
- step_sizes: float32 [112], replicated, may hold values from 0.02 to 0.1
- modulation: bfloat16 [112, 10, 1536], replicated, may hold values from -4 to 4
- context: bfloat16 [128, 1536], replicated, may hold values from -6 to 6
- position_embed: bfloat16 [128, 1536], P('tp'), may hold values from -2 to 2
- patch_weight: bfloat16 [64, 1536], replicated, may hold values from -0.75 to 0.75
- heads_weight: bfloat16 [1536, 3, 1536], P(None, None, 'tp'), may hold values from -0.15625 to 0.15625
- query_gain: float32 [64], replicated, may hold values from 0.1 to 1.9
- key_gain: float32 [64], replicated, may hold values from 0.1 to 1.9
- text_weight: bfloat16 [1536, 2, 1536], P(None, None, 'tp'), may hold values from -0.15625 to 0.15625
- output_weight: bfloat16 [1536, 1536], P('tp'), may hold values from -0.15625 to 0.15625
- up_weight: bfloat16 [1536, 6144], P(None, 'tp'), may hold values from -0.15625 to 0.15625
- down_weight: bfloat16 [6144, 1536], P('tp'), may hold values from -0.078125 to 0.078125
- final_weight: bfloat16 [1536, 64], replicated, may hold values from -0.15625 to 0.15625
Outputs:
- trajectory_next: float32 [64, 128, 64], P('tm', 'tp')
The draws below stay inside these ranges and needn't reach their ends.
All inputs are finite; a program needn't handle non-finite values.
Results may differ from the reference program's by a relative error of at most 0.0085.
Values may be sent and summed in bfloat16 or wider, within the bound.
A program may use at most 64 MiB of HBM per device.

```python
import math
import jax
import jax.numpy as jnp
from jax import lax

D = 1536
HEADS = 24
HD = 64
FF = 6144
PATCH = 64
SEQ = 128
TXT = 128
TS_DEV = 2
ITERS = 3
TW = 64
TABLE = 112


def level_of(rng, dims, split, low, largest):
    def one(axis_at, parts):
        heights = jax.random.uniform(jax.random.fold_in(jax.random.fold_in(rng, 6), axis_at), (parts,), jnp.float32, low / len(split), largest / len(split))
        return jnp.repeat(jnp.exp(heights), dims[axis_at] // parts).reshape((-1,) + (1,) * (len(dims) - axis_at - 1))

    gain = one(*split[0])
    for cut in split[1:]:
        gain = gain * one(*cut)
    return gain


def centred(own_key, extent, scale, bound, split=(), dtype=jnp.bfloat16):
    array = scale * jax.random.normal(own_key, extent, jnp.float32)
    if split:
        array = array * level_of(own_key, extent, split, -0.22, 0.18)
    return jnp.clip(array, -bound, bound).astype(dtype)


def setup_inputs(seed: int = 0) -> dict:
    arg_keys = jax.random.split(jax.random.key(seed), 16)
    trajectory = centred(arg_keys[0], (TW, SEQ, PATCH), 1.0, 6.0, ((0, 32), (1, 8)), jnp.float32)
    window_start = jax.random.randint(arg_keys[1], (1,), 0, 24 * TS_DEV + 1).astype(jnp.int32)
    step_sizes = jnp.clip(jnp.exp(jax.random.uniform(arg_keys[2], (TABLE,), jnp.float32, math.log(0.02), math.log(0.1))), 0.02, 0.1)
    modulation = centred(arg_keys[3], (TABLE, 10, D), 1.0, 4.0)
    context = centred(arg_keys[4], (TXT, D), 1.0, 6.0)
    position_embed = centred(arg_keys[5], (SEQ, D), 0.3, 2.0, ((0, 8),))
    patch_weight = centred(arg_keys[6], (PATCH, D), PATCH ** -0.5, 0.75)
    heads_weight = centred(arg_keys[7], (D, 3, D), D ** -0.5, 0.15625, ((2, 8),))
    query_gain = jnp.clip(1.0 + 0.18 * jax.random.normal(arg_keys[8], (HD,), jnp.float32), 0.1, 1.9)
    key_gain = jnp.clip(1.0 + 0.18 * jax.random.normal(arg_keys[9], (HD,), jnp.float32), 0.1, 1.9)
    text_weight = centred(arg_keys[10], (D, 2, D), D ** -0.5, 0.15625, ((2, 8),))
    output_weight = centred(arg_keys[11], (D, D), D ** -0.5, 0.15625, ((0, 8),))
    up_weight = centred(arg_keys[12], (D, FF), D ** -0.5, 0.15625, ((1, 8),))
    down_weight = centred(arg_keys[13], (FF, D), FF ** -0.5, 0.078125, ((0, 8),))
    final_weight = centred(arg_keys[14], (D, PATCH), D ** -0.5, 0.15625)
    return {"trajectory": trajectory, "window_start": window_start, "step_sizes": step_sizes, "modulation": modulation, "context": context, "position_embed": position_embed, "patch_weight": patch_weight, "heads_weight": heads_weight, "query_gain": query_gain, "key_gain": key_gain, "text_weight": text_weight, "output_weight": output_weight, "up_weight": up_weight, "down_weight": down_weight, "final_weight": final_weight}


EPSILON = 1e-06

def layer_norm(values):
    average = lax.optimization_barrier(jnp.mean(values, axis=-1, keepdims=True))
    centered = values - average
    spread = lax.optimization_barrier(jnp.mean(centered * centered, axis=-1, keepdims=True))
    return centered * lax.rsqrt(spread + EPSILON)

def modulate(values, shift_by, scale_by):
    return (layer_norm(values) * (1.0 + scale_by) + shift_by).astype(jnp.bfloat16)

def head_norm(values, gain_vector):
    square = lax.optimization_barrier(jnp.mean(values * values, axis=-1, keepdims=True))
    return (values * lax.rsqrt(square + EPSILON) * gain_vector).astype(jnp.bfloat16)

def drift_one(states, table_rows, context, position_embed, patch_weight, heads_weight, query_gain, key_gain, text_weight, output_weight, up_weight, down_weight, final_weight):
    hidden = jnp.dot(states.astype(jnp.bfloat16), patch_weight, preferred_element_type=jnp.float32) + position_embed.astype(jnp.float32)
    normed = modulate(hidden, table_rows[0], table_rows[1])
    joint = jnp.dot(normed, heads_weight.reshape(D, 3 * D), preferred_element_type=jnp.float32)
    query = head_norm(joint[:, :D].reshape(SEQ, HEADS, HD), query_gain)
    image_keys = head_norm(joint[:, D:2 * D].reshape(SEQ, HEADS, HD), key_gain)
    image_values = joint[:, 2 * D:].astype(jnp.bfloat16).reshape(SEQ, HEADS, HD)
    text_normed = modulate(context.astype(jnp.float32), table_rows[6], table_rows[7])
    text_joint = jnp.dot(text_normed, text_weight.reshape(D, 2 * D), preferred_element_type=jnp.float32)
    text_keys = head_norm(text_joint[:, :D].reshape(TXT, HEADS, HD), key_gain)
    text_values = text_joint[:, D:].astype(jnp.bfloat16).reshape(TXT, HEADS, HD)
    all_keys = jnp.concatenate([image_keys, text_keys], axis=0).astype(jnp.float32)
    all_values = jnp.concatenate([image_values, text_values], axis=0).astype(jnp.float32)
    scores = jnp.einsum('qhd,khd->hqk', query.astype(jnp.float32), all_keys) * HD ** (-0.5)
    powers = jnp.exp(scores)
    probs = (powers / lax.optimization_barrier(jnp.sum(powers, axis=-1, keepdims=True))).astype(jnp.bfloat16)
    attended = jnp.einsum('hqk,khd->qhd', probs.astype(jnp.float32), all_values).astype(jnp.bfloat16).reshape(SEQ, D)
    hidden = hidden + table_rows[2] * jnp.dot(attended, output_weight, preferred_element_type=jnp.float32)
    normed = modulate(hidden, table_rows[3], table_rows[4])
    activated = jax.nn.gelu(jnp.dot(normed, up_weight, preferred_element_type=jnp.float32), approximate=True).astype(jnp.bfloat16)
    hidden = hidden + table_rows[5] * jnp.dot(activated, down_weight, preferred_element_type=jnp.float32)
    final_normed = modulate(hidden, table_rows[8], table_rows[9])
    return jnp.dot(final_normed, final_weight, preferred_element_type=jnp.float32)

def reference(trajectory, window_start, step_sizes, modulation, context, position_embed, patch_weight, heads_weight, query_gain, key_gain, text_weight, output_weight, up_weight, down_weight, final_weight):
    first_entry = window_start[0].astype(jnp.int32)
    window_steps = lax.dynamic_slice_in_dim(step_sizes, first_entry, TW)
    window_table = lax.dynamic_slice_in_dim(modulation, first_entry, TW).astype(jnp.float32)
    anchor = trajectory[0]

    def evaluate(paired):
        return drift_one(paired[0], paired[1], context, position_embed, patch_weight, heads_weight, query_gain, key_gain, text_weight, output_weight, up_weight, down_weight, final_weight)
    states = trajectory
    outcome = trajectory
    for repeat in range(ITERS):
        drifts = lax.map(evaluate, (states, window_table))
        terms = window_steps[:, None, None] * drifts
        inclusive = jnp.cumsum(terms, axis=0)
        exclusive = jnp.concatenate([jnp.zeros_like(terms[:1]), inclusive[:-1]], axis=0)
        states = anchor[None] - exclusive
        outcome = anchor[None] - inclusive
    return outcome
```

```python
import functools

import jax
import jax.numpy as jnp
from jax import lax
from jax.experimental import pallas as pl
from jax.experimental.pallas import tpu as pltpu
from jax.sharding import PartitionSpec as P

ROUNDS = 3
EPSILON = 1e-06
MESH = pl.DeviceIdType.MESH
F32 = jnp.float32
BF16 = jnp.bfloat16

CHUNKS = 12
CHUNK = 192
PIECE = 48
HEAD_ROWS, WO_AT, UP_AT, DOWN_AT, ALL_ROWS = 576, 576, 768, 1536, 2304


def nt(a, b):
    return lax.dot_general(a, b, (((1,), (1,)), ((), ())), preferred_element_type=F32)


def nn(a, b):
    return jnp.dot(a, b, preferred_element_type=F32)


def ln_mod(values, shift, scale):
    average = jnp.mean(values, axis=-1, keepdims=True)
    centered = values - average
    spread = jnp.mean(centered * centered, axis=-1, keepdims=True)
    return (centered * lax.rsqrt(spread + EPSILON) * (1.0 + scale) + shift).astype(BF16)


def ln_rows(source, target, shift, scale, rows):
    def block(i, carry):
        at = pl.ds(pl.multiple_of(i * 16, 16), 16)
        target[at, :] = ln_mod(source[at, :].astype(F32), shift, scale)
        return carry

    lax.fori_loop(0, rows // 16, block, 0, unroll=2)


def head_norm_t(values, gain):
    split = values.reshape(values.shape[0] // 64, 64, values.shape[1])
    square = jnp.mean(split * split, axis=1, keepdims=True)
    return split * lax.rsqrt(square + EPSILON) * gain[None]


def device(z, x, core, y):
    z, x, y = (z + 8) % 8, (x + 4) % 4, (y + 4) % 4
    return (((z % 4) * 4 + x) * 2 + core, y * 2 + z // 4)


def kernel(
    traj, mods, steps, ctx, pos, patch, heads, q_gain, k_gain, text, wo, up, down, final,
    out,
    WB, WOF, TT, POS, XIN, XR, TN, CKN, CVT, CSEND, CRECV, H, N, ACC, AB, RSS, RSB,
    TS, US, SX, TEI, SZT, SZE,
    local, zs, zr, xs, xr, cs, cr, wos, wor, wfs, wfr,
    exs, exr, gs, gr, txs, txr, ats, atr, rss, rsr, us, ur, sxs, sxr, szs, szr,
):
    tm, tp = lax.axis_index("tm"), lax.axis_index("tp")
    zl, x, core = tm // 8, (tm // 2) % 4, tm % 2
    y, zh = tp // 2, tp % 2
    z = zh * 4 + zl
    way = 1 - 2 * core

    def copy(src, dst, send, recv, to):
        return pltpu.make_async_remote_copy(
            src_ref=src, dst_ref=dst, send_sem=send, recv_sem=recv, device_id=to, device_id_type=MESH
        )

    y_peers = [device(z, x, core, y + k) for k in (1, 2, 3)]
    x_peers = [device(z, x + k, core, y) for k in (1, 2, 3)]
    z_peers = [device(z + k, x, core, y) for k in range(1, 8)]
    other_core = device(z, x, 1 - core, y)
    other_half = device(z + 4, x, core, y)

    loads = [
        pltpu.make_async_copy(heads, WB.at[0, pl.ds(0, HEAD_ROWS)], local.at[0]),
        pltpu.make_async_copy(wo, WB.at[0, pl.ds(WO_AT, 192)], local.at[1]),
        pltpu.make_async_copy(
            up.at[pl.ds(0, 768)], WB.at[0, pl.ds(UP_AT, 768), pl.ds(0, 768)], local.at[2]
        ),
        pltpu.make_async_copy(
            up.at[pl.ds(768, 768)], WB.at[0, pl.ds(UP_AT, 768), pl.ds(768, 768)], local.at[3]
        ),
        pltpu.make_async_copy(down, WB.at[0, pl.ds(DOWN_AT, 768)], local.at[4]),
        pltpu.make_async_copy(text, TT, local.at[5]),
        pltpu.make_async_copy(wo, WOF.at[y, 0], local.at[6]),
    ]
    for load in loads:
        load.start()

    barrier = pltpu.get_barrier_semaphore()
    everyone = y_peers + x_peers + z_peers + [other_core]
    for peer in everyone:
        pl.semaphore_signal(barrier, inc=1, device_id=peer, device_id_type=MESH)
    pl.semaphore_wait(barrier, len(everyone))

    half = pl.ds(pl.multiple_of(zh * 16, 16), 16)
    ex_x = copy(traj.at[1 - zh], XR.at[zh], exs.at[0], exr.at[0], other_half)
    ex_pos = copy(pos, POS.at[y, half], exs.at[1], exr.at[1], other_half)
    ex_x.start()
    ex_pos.start()
    XR[zh] = traj[zh]
    POS[y, half, :] = pos[...]

    even = x % 2
    first = jnp.where(core == 0, zl == 3, zl == 0)
    own = 1 - first.astype(jnp.int32)
    z_quarter = 2 * core + even
    x_quarter = 2 * core + 1 - even

    def rows(quarter, c):
        return pl.ds(pl.multiple_of(c * CHUNK + quarter * PIECE, 16), PIECE)

    def z_copy(c):
        at = rows(z_quarter, c)
        return copy(
            WB.at[own, at], WB.at[1, at], zs.at[c], zr.at[c], device(z + way, x, core, y)
        )

    def x_copy(c):
        at = rows(z_quarter, c)
        return copy(WB.at[1, at], WB.at[1, at], xs.at[c], xr.at[c], device(z, x + way, core, y))

    def core_copy(k, quarter, c):
        at = rows(quarter, c)
        return copy(WB.at[1, at], WB.at[1, at], cs.at[k, c], cr.at[k, c], other_core)

    for load in loads[:5]:
        load.wait()

    @pl.when(first)
    def _():
        def send(c, carry):
            z_copy(c).start()
            return carry

        lax.fori_loop(0, CHUNKS, send, 0)

    def pump_x(c):
        x_copy(c).wait_recv()
        core_copy(1, x_quarter, c).start()

    def pump(c, carry):
        z_copy(c).wait_recv()

        @pl.when(jnp.logical_not(first))
        def _():
            z_copy(c).start()

        x_copy(c).start()
        core_copy(0, z_quarter, c).start()

        @pl.when(c > 0)
        def _():
            pump_x(c - 1)

        return carry

    def arrive(c, carry):
        core_copy(0, z_quarter, c).wait_recv()
        core_copy(1, x_quarter, c).wait_recv()
        return carry

    mine = pl.ds(pl.multiple_of(core * 96, 16), 96)

    def wo_copies(part):
        return [
            copy(
                WB.at[part, pl.ds(pl.multiple_of(WO_AT + core * 96, 16), 96)],
                WOF.at[y, part, mine],
                wos.at[part, k],
                wor.at[part, k],
                y_peers[k],
            )
            for k in range(3)
        ]

    def wo_forwards(part):
        return [
            copy(
                WOF.at[(y + 3 - k) % 4, part, mine],
                WOF.at[(y + 3 - k) % 4, part, mine],
                wfs.at[part, k],
                wfr.at[part, k],
                other_core,
            )
            for k in range(3)
        ]

    ex_x.wait()
    ex_pos.wait()
    XIN[0, y, 0:16, :] = XR[0].astype(BF16)
    XIN[0, y, 16:32, :] = XR[1].astype(BF16)

    def state_copies(r):
        return [
            copy(XIN.at[r, y], XIN.at[r, y], gs.at[r, k], gr.at[r, k], y_peers[k])
            for k in range(3)
        ]

    pos_copies = [
        copy(POS.at[y], POS.at[y], gs.at[3, k], gr.at[3, k], y_peers[k]) for k in range(3)
    ]
    for one in state_copies(0) + pos_copies:
        one.start()
    for one in wo_copies(0):
        one.start()

    pump(0, 0)

    loads[5].wait()
    loads[6].wait()

    def prompt(slot):
        ln_rows(ctx, TN, mods[slot, 6:7, :], mods[slot, 7:8, :], 128)
        joint = nt(TT[...], TN[...])
        keys = head_norm_t(joint[:192], k_gain[...]).reshape(192, 128)
        return keys, joint[192:].astype(BF16)

    keys, values = prompt(1 - zh)
    CSEND[0:192, :] = keys.astype(BF16)
    CSEND[192:384, :] = values
    text_copy = copy(CSEND, CRECV, txs, txr, other_half)
    text_copy.start()
    pump(1, 0)
    keys, values = prompt(zh)
    for i in range(3):
        CKN[0, i] = keys[i * 64 : (i + 1) * 64].T.astype(BF16)
    CVT[0] = values
    pump(2, 0)

    hop = jnp.where(core == 0, zl + 1, 4 - zl)
    before = jnp.where(hop == 1, 12, jnp.where(hop == 2, 10, jnp.where(hop == 3, 7, 5)))
    lax.fori_loop(3, before, pump, 0)

    text_copy.wait()
    for i in range(3):
        CKN[1, i] = CRECV[i * 64 : (i + 1) * 64, :].astype(F32).T.astype(BF16)
    CVT[1] = CRECV[192:384, :]
    for one in state_copies(0) + pos_copies:
        one.wait()
    lax.fori_loop(0, 3, arrive, 0)

    own_rows = pl.ds(pl.multiple_of(y * 32, 32), 32)
    start_slot = jnp.logical_and(tm == 0, zh == 0)

    def mod(k):
        return mods[zh, k : k + 1, :]

    def one_round(r, carry):
        X = XIN[r].reshape(128, 64)
        H[...] = nn(X, patch[...]) + POS[...].reshape(128, 1536).astype(F32)
        ln_rows(H, N, mod(0), mod(1), 128)

        parts = []
        for s in range(2):
            joint = nt(WB[s, 0:HEAD_ROWS, :], N[...])
            query = head_norm_t(joint[:192], q_gain[...]).astype(BF16)
            keys = head_norm_t(joint[192:384], k_gain[...])
            values = joint[384:].astype(BF16)
            for i in range(3):
                key_rows = jnp.concatenate([keys[i].T.astype(BF16), CKN[s, i]], axis=0)
                scores = nn(key_rows, query[i]) * 0.125
                powers = jnp.exp(scores)
                probs = (powers / jnp.sum(powers, axis=0, keepdims=True)).astype(BF16)
                both = jnp.concatenate(
                    [values[i * 64 : (i + 1) * 64], CVT[s, i * 64 : (i + 1) * 64, :]], axis=1
                )
                parts.append(nn(both, probs))
        AB[r, y] = jnp.concatenate(parts, axis=0).T.astype(BF16)
        attended = [
            copy(AB.at[r, y], AB.at[r, y], ats.at[r, k], atr.at[r, k], y_peers[k])
            for k in range(3)
        ]
        for one in attended:
            one.start()

        @pl.when(r == 0)
        def _():
            for one, forward in zip(wo_copies(0), wo_forwards(0)):
                one.wait_recv()
                forward.start()
            lax.fori_loop(before, CHUNKS, pump, 0)
            pump_x(CHUNKS - 1)
            for one in wo_copies(1):
                one.start()
            lax.fori_loop(3, CHUNKS, arrive, 0)
            fill = pltpu.make_async_copy(
                WB.at[1, pl.ds(WO_AT, 192)], WOF.at[y, 1], local.at[7]
            )
            fill.start()
            for one, forward in zip(wo_copies(1), wo_forwards(1)):
                one.wait_recv()
                forward.start()
            fill.wait()
            for part in range(2):
                for forward in wo_forwards(part):
                    forward.wait_recv()

        def project(k):
            return nn(AB[r, (y + k) % 4], WOF[(y + k) % 4].reshape(384, 1536))

        ACC[...] = project(0)
        for k, one in ((1, attended[2]), (3, attended[0]), (2, attended[1])):
            one.wait_recv()
            ACC[...] += project(k)
        H[...] = H[...] + mod(2) * ACC[...]
        ln_rows(H, N, mod(3), mod(4), 128)

        total = None
        for s in range(2):
            hidden = nn(N[:, 0:768], WB[s, UP_AT:DOWN_AT, 0:768]) + nn(
                N[:, 768:1536], WB[s, UP_AT:DOWN_AT, 768:1536]
            )
            active = jax.nn.gelu(hidden, approximate=True).astype(BF16)
            part = nn(active, WB[s, DOWN_AT:ALL_ROWS, :])
            total = part if total is None else total + part
        ACC[...] = total
        RSS[...] = total.astype(BF16)
        summed = [
            copy(
                RSS.at[pl.ds(pl.multiple_of(((y + k + 1) % 4) * 32, 32), 32)],
                RSB.at[r, k],
                rss.at[r, k],
                rsr.at[r, k],
                y_peers[k],
            )
            for k in range(3)
        ]
        for one in summed:
            one.start()
        for one in summed:
            one.wait_recv()
        contract = ACC[own_rows, :]
        for k in range(3):
            contract = contract + RSB[r, k].astype(F32)
        state = ln_mod(H[own_rows, :] + mod(5) * contract, mod(8), mod(9))
        term = steps[zh] * nt(state, final[...])
        anchor = jnp.concatenate([XR[0], XR[1]], axis=0)
        term = term - jnp.where(start_slot, anchor, jnp.zeros_like(anchor))

        TS[r] = term
        pair = copy(TS.at[r], US.at[r], us.at[r], ur.at[r], other_core)
        pair.start()
        pair.wait_recv()
        chip = term + US[r]
        SX[r, x] = chip
        along_x = [
            copy(SX.at[r, x], SX.at[r, x], sxs.at[r, k], sxr.at[r, k], x_peers[k])
            for k in range(3)
        ]
        for one in along_x:
            one.start()
        for one in along_x:
            one.wait_recv()
        before_me = jnp.where(core == 1, US[r], jnp.zeros_like(term))
        whole = jnp.zeros_like(term)
        for i in range(4):
            block = SX[r, i]
            whole = whole + block
            before_me = before_me + jnp.where(i < x, block, jnp.zeros_like(block))
        TEI[r, 0] = whole
        TEI[r, 1] = before_me
        TEI[r, 2] = before_me + term
        SZT[r, z] = whole
        along_z = [
            copy(TEI.at[r, pl.ds(1, 2)], SZE.at[r], szs.at[r, 7], szr.at[r, 7], other_half)
        ] + [
            copy(TEI.at[r, 0], SZT.at[r, z], szs.at[r, k - 1], szr.at[r, k - 1], z_peers[k - 1])
            for k in (4, 3, 5, 2, 6, 1, 7)
        ]
        for one in along_z:
            one.start()
        for one in along_z:
            one.wait_recv()
        base = jnp.zeros_like(term)
        for i in range(8):
            block = SZT[r, i]
            base = base + jnp.where(i % 4 < zl, block, jnp.zeros_like(block))
        upper = zh == 1
        earlier = base + before_me + jnp.where(upper, SZE[r, 1], SZE[r, 0])

        @pl.when(r < ROUNDS - 1)
        def _():
            fresh = jnp.where(start_slot, anchor, -earlier)
            XIN[r + 1, y] = fresh.astype(BF16)
            for one in state_copies(r + 1):
                one.start()
            for one in state_copies(r + 1):
                one.wait()

        @pl.when(r == ROUNDS - 1)
        def _():
            ACC[0:32, 0:64] = -(earlier + term)
            ACC[32:64, 0:64] = -(
                base + SZE[r, 1] + jnp.where(upper, before_me, before_me + term)
            )
            out[zh] = ACC[half, 0:64]
            out[1 - zh] = ACC[pl.ds(pl.multiple_of(32 + zh * 16, 16), 16), 0:64]

        for one in attended + summed + [pair] + along_x + along_z:
            one.wait_send()
        return carry

    lax.fori_loop(0, ROUNDS, one_round, 0)

    def drain(c, carry):
        z_copy(c).wait_send()
        x_copy(c).wait_send()
        core_copy(0, z_quarter, c).wait_send()
        core_copy(1, x_quarter, c).wait_send()
        return carry

    lax.fori_loop(0, CHUNKS, drain, 0)
    for part in range(2):
        for one in wo_copies(part) + wo_forwards(part):
            one.wait_send()


def per_device(
    trajectory,
    window_start,
    step_sizes,
    modulation,
    context,
    position_embed,
    patch_weight,
    heads_weight,
    query_gain,
    key_gain,
    text_weight,
    output_weight,
    up_weight,
    down_weight,
    final_weight,
):
    entry = window_start[0] + lax.axis_index("tm") * 2
    table = lax.dynamic_slice_in_dim(modulation, entry, 2).astype(F32)
    steps = lax.dynamic_slice_in_dim(step_sizes, entry, 2)
    steps = jnp.broadcast_to(steps[:, None, None], (2, 1, 64))
    heads = heads_weight.transpose(1, 2, 0).reshape(HEAD_ROWS, 1536)
    text = text_weight.transpose(1, 2, 0).reshape(384, 1536)
    vmem = pl.BlockSpec(memory_space=pltpu.VMEM)
    hbm = pl.BlockSpec(memory_space=pl.ANY)
    dma = pltpu.SemaphoreType.DMA
    R = ROUNDS
    return pl.pallas_call(
        kernel,
        out_shape=jax.ShapeDtypeStruct((2, 16, 64), F32),
        in_specs=[vmem] * 6 + [hbm, vmem, vmem, hbm, hbm, hbm, hbm, vmem],
        out_specs=vmem,
        scratch_shapes=[
            pltpu.VMEM((2, ALL_ROWS, 1536), BF16),
            pltpu.VMEM((4, 2, 192, 1536), BF16),
            pltpu.VMEM((384, 1536), BF16),
            pltpu.VMEM((4, 32, 1536), BF16),
            pltpu.VMEM((R, 4, 32, 64), BF16),
            pltpu.VMEM((2, 16, 64), F32),
            pltpu.VMEM((128, 1536), BF16),
            pltpu.VMEM((2, 3, 128, 64), BF16),
            pltpu.VMEM((2, 192, 128), BF16),
            pltpu.VMEM((384, 128), BF16),
            pltpu.VMEM((384, 128), BF16),
            pltpu.VMEM((128, 1536), F32),
            pltpu.VMEM((128, 1536), BF16),
            pltpu.VMEM((128, 1536), F32),
            pltpu.VMEM((R, 4, 128, 384), BF16),
            pltpu.VMEM((128, 1536), BF16),
            pltpu.VMEM((R, 3, 32, 1536), BF16),
            pltpu.VMEM((R, 32, 64), F32),
            pltpu.VMEM((R, 32, 64), F32),
            pltpu.VMEM((R, 4, 32, 64), F32),
            pltpu.VMEM((R, 3, 32, 64), F32),
            pltpu.VMEM((R, 8, 32, 64), F32),
            pltpu.VMEM((R, 2, 32, 64), F32),
            dma((8,)),
            dma((CHUNKS,)),
            dma((CHUNKS,)),
            dma((CHUNKS,)),
            dma((CHUNKS,)),
            dma((2, CHUNKS)),
            dma((2, CHUNKS)),
            dma((2, 3)),
            dma((2, 3)),
            dma((2, 3)),
            dma((2, 3)),
            dma((2,)),
            dma((2,)),
            dma((4, 3)),
            dma((4, 3)),
            dma,
            dma,
            dma((R, 3)),
            dma((R, 3)),
            dma((R, 3)),
            dma((R, 3)),
            dma((R,)),
            dma((R,)),
            dma((R, 3)),
            dma((R, 3)),
            dma((R, 8)),
            dma((R, 8)),
        ],
        compiler_params=pltpu.CompilerParams(
            collective_id=0, has_side_effects=True, vmem_limit_bytes=56 << 20
        ),
        cost_estimate=pl.CostEstimate(
            flops=7_000_000_000, bytes_accessed=10_000_000, transcendentals=1_000_000
        ),
        name="picard",
    )(
        trajectory,
        table,
        steps,
        context,
        position_embed,
        patch_weight,
        heads,
        query_gain[:, None],
        key_gain[:, None],
        text,
        output_weight,
        up_weight,
        down_weight,
        final_weight.T,
    )


def solution(mesh):
    return jax.shard_map(
        per_device,
        mesh=mesh,
        in_specs=(
            P("tm", "tp", None),
            P(),
            P(),
            P(),
            P(),
            P("tp", None),
            P(),
            P(None, None, "tp"),
            P(),
            P(),
            P(None, None, "tp"),
            P("tp", None),
            P(None, "tp"),
            P("tp", None),
            P(),
        ),
        out_specs=P("tm", "tp", None),
        check_vma=False,
    )
```

```python
import functools

import jax
import jax.numpy as jnp
from jax import lax
from jax.experimental import pallas as pl
from jax.experimental.pallas import tpu as pltpu
from jax.sharding import PartitionSpec as P

ROUNDS = 3
EPSILON = 1e-06
MESH = pl.DeviceIdType.MESH
F32 = jnp.float32
BF16 = jnp.bfloat16

LAG = 3
CHUNKS = 12
CHUNK = 192
STEPS = CHUNKS + LAG
PIECE = 48
HEAD_ROWS = 576
WO_AT, HEADS_AT, UP_AT, DOWN_AT, ALL_ROWS = 0, 192, 768, 1536, 2304


def nt(a, b):
    return lax.dot_general(a, b, (((1,), (1,)), ((), ())), preferred_element_type=F32)


def nn(a, b):
    return jnp.dot(a, b, preferred_element_type=F32)


def ln_mod(values, shift, scale):
    average = jnp.mean(values, axis=-1, keepdims=True)
    centered = values - average
    spread = jnp.mean(centered * centered, axis=-1, keepdims=True)
    return (centered * lax.rsqrt(spread + EPSILON) * (1.0 + scale) + shift).astype(BF16)


def ln_rows(source, target, shift, scale, start, rows):
    def block(i, carry):
        at = pl.ds(pl.multiple_of(start + i * 16, 16), 16)
        target[at, :] = ln_mod(source[at, :].astype(F32), shift, scale)
        return carry

    lax.fori_loop(0, rows // 16, block, 0, unroll=2)


def head_norm_t(values, gain):
    split = values.reshape(values.shape[0] // 64, 64, values.shape[1])
    square = jnp.mean(split * split, axis=1, keepdims=True)
    return split * lax.rsqrt(square + EPSILON) * gain[None]


def device(z, x, core, y):
    z, x, y = (z + 8) % 8, (x + 4) % 4, (y + 4) % 4
    return (((z % 4) * 4 + x) * 2 + core, y * 2 + z // 4)


def kernel(
    traj, start, steps, table, ctx, pos, patch, heads, q_gain, k_gain, text, wo, up, down, final,
    out,
    WB, WOF, TT, POS, XIN, XR, TN, CKN, CVT, CS, CRECV, H, N, ACC, AB, RSS, RSB,
    TZ, SUMS, XS, TABLE, MODS, CTX, PATCH, FINAL, GAINS,
    local, zs, zr, xs, xr, cs, cr, wos, wor, wfs, wfr,
    exs, exr, gs, gr, txs, txr, ats, atr, rss, rsr, sxs, sxr, szs, szr,
):
    tm, tp = lax.axis_index("tm"), lax.axis_index("tp")
    zl, x, core = tm // 8, (tm // 2) % 4, tm % 2
    y, zh = tp // 2, tp % 2
    z = zh * 4 + zl
    way = 1 - 2 * core

    def copy(src, dst, send, recv, to):
        return pltpu.make_async_remote_copy(
            src_ref=src, dst_ref=dst, send_sem=send, recv_sem=recv, device_id=to, device_id_type=MESH
        )

    y_peers = [device(z, x, core, y + k) for k in (1, 2, 3)]
    z_peers = [device(z + k, x, core, y) for k in range(1, 8)]
    other_core = device(z, x, 1 - core, y)
    other_half = device(z + 4, x, core, y)

    barrier = pltpu.get_barrier_semaphore()
    x_peers = [device(z, x + k // 2, (core + k) % 2, y) for k in range(1, 8)]
    everyone = y_peers + x_peers + z_peers
    for peer in everyone:
        pl.semaphore_signal(barrier, inc=1, device_id=peer, device_id_type=MESH)

    loads = [
        pltpu.make_async_copy(src, dst, local.at[i])
        for i, (src, dst) in enumerate(
            [
                (wo, WB.at[0, pl.ds(WO_AT, 192)]),
                (heads, WB.at[0, pl.ds(HEADS_AT, HEAD_ROWS)]),
                (up.at[pl.ds(0, 768)], WB.at[0, pl.ds(UP_AT, 768), pl.ds(0, 768)]),
                (up.at[pl.ds(768, 768)], WB.at[0, pl.ds(UP_AT, 768), pl.ds(768, 768)]),
                (down, WB.at[0, pl.ds(DOWN_AT, 768)]),
                (table, TABLE),
                (ctx, CTX),
                (text, TT),
                (patch, PATCH),
                (wo, WOF.at[y, 0]),
                (final, FINAL),
            ]
        )
    ]
    for i in (5, 0, 1, 2, 3, 4, 6, 7, 8, 9, 10):
        loads[i].start()

    entry = start[0] + tm * 2
    line = lax.broadcasted_iota(jnp.int32, (8, 112), 0)
    wanted = entry + jnp.where(line == 0, zh, 1 - zh)
    pick = (lax.broadcasted_iota(jnp.int32, (8, 112), 1) == wanted).astype(F32)
    step = jnp.sum(pick[0:1] * steps[...], axis=1, keepdims=True)
    pick = pick.astype(BF16)
    loads[5].wait()
    for k in range(10):
        MODS[k] = nn(pick, TABLE[k])
    GAINS[0] = jnp.broadcast_to(q_gain[...], (128, 64)).T
    GAINS[1] = jnp.broadcast_to(k_gain[...], (128, 64)).T

    pl.semaphore_wait(barrier, len(everyone))

    half = pl.ds(pl.multiple_of(zh * 16, 16), 16)
    ex_x = copy(traj.at[1 - zh], XR.at[zh], exs.at[0], exr.at[0], other_half)
    ex_pos = copy(pos, POS.at[y, half], exs.at[1], exr.at[1], other_half)
    ex_x.start()
    ex_pos.start()
    XR[zh] = traj[zh]
    POS[y, half, :] = pos[...]

    even = x % 2
    first = jnp.where(core == 0, zl == 3, zl == 0)
    own = 1 - first.astype(jnp.int32)
    z_quarter = 2 * core + even

    def rows(quarter, c):
        return pl.ds(pl.multiple_of(c * CHUNK + quarter * PIECE, 16), PIECE)

    def z_copy(c):
        at = rows(z_quarter, c)
        return copy(
            WB.at[own, at], WB.at[1, at], zs.at[c], zr.at[c], device(z + way, x, core, y)
        )

    def x_copy(c):
        at = rows(z_quarter, c)
        return copy(WB.at[1, at], WB.at[1, at], xs.at[c], xr.at[c], device(z, x + way, core, y))

    def core_copy(c):
        at = pl.ds(pl.multiple_of(c * CHUNK + core * 2 * PIECE, 16), 2 * PIECE)
        return copy(WB.at[1, at], WB.at[1, at], cs.at[c], cr.at[c], other_core)

    for load in loads[0:5]:
        load.wait()

    @pl.when(first)
    def _():
        def send(c, carry):
            z_copy(c).start()
            return carry

        lax.fori_loop(0, CHUNKS, send, 0)

    def pump_x(c):
        x_copy(c).wait_recv()
        core_copy(c).start()

    def pump(c, carry):
        @pl.when(c < CHUNKS)
        def _():
            z_copy(c).wait_recv()

            @pl.when(jnp.logical_not(first))
            def _():
                z_copy(c).start()

            x_copy(c).start()

        @pl.when(c >= LAG)
        def _():
            pump_x(c - LAG)

        @pl.when(c == LAG)
        def _():
            for one in wo_copies(1):
                one.start()

        return carry

    def arrive(c, carry):
        core_copy(c).wait_recv()
        return carry

    mine = pl.ds(pl.multiple_of(core * 96, 16), 96)

    def wo_copies(part):
        return [
            copy(
                WB.at[part, pl.ds(pl.multiple_of(WO_AT + core * 96, 16), 96)],
                WOF.at[y, part, mine],
                wos.at[part, k],
                wor.at[part, k],
                y_peers[k],
            )
            for k in range(3)
        ]

    def wo_forwards(part):
        return [
            copy(
                WOF.at[(y + 3 - k) % 4, part, mine],
                WOF.at[(y + 3 - k) % 4, part, mine],
                wfs.at[part, k],
                wfr.at[part, k],
                other_core,
            )
            for k in range(3)
        ]

    loads[6].wait()
    loads[7].wait()
    text_copy = copy(CS.at[1 - zh], CRECV, txs, txr, other_half)

    def prompt(c):
        of_other = c < 6
        slot = jnp.where(of_other, 1 - zh, zh)
        part = c % 6

        @pl.when(part < 4)
        def _():
            shift, scale = (
                jnp.where(of_other, MODS[k, 1:2, :], MODS[k, 0:1, :]) for k in (6, 7)
            )
            ln_rows(CTX, TN, shift, scale, part * 32, 32)

        @pl.when(part == 4)
        def _():
            keys = head_norm_t(nt(TT[0:192, :], TN[...]), GAINS[1])
            CS[slot, 0:192, :] = keys.reshape(192, 128).astype(BF16)

        @pl.when(part == 5)
        def _():
            CS[slot, 192:384, :] = nt(TT[192:384, :], TN[...]).astype(BF16)

        @pl.when(c == 5)
        def _():
            text_copy.start()

    def only_prompt(c, carry):
        prompt(c)
        return carry

    hop = jnp.where(core == 0, zl + 1, 4 - zl)

    def by_hop(*values):
        return jnp.where(
            hop == 1,
            values[0],
            jnp.where(hop == 2, values[1], jnp.where(hop == 3, values[2], values[3])),
        )

    ready, before, middle = by_hop(0, 6, 12, 12), by_hop(15, 14, 9, 7), by_hop(15, 15, 15, 10)
    lax.fori_loop(0, ready, only_prompt, 0)
    pump(0, 0)

    ex_x.wait()
    ex_pos.wait()
    anchor = jnp.concatenate([XR[0], XR[1]], axis=1)
    XIN[0, y] = anchor.astype(BF16)

    def state_copies(r):
        return [
            copy(XIN.at[r, y], XIN.at[r, y], gs.at[r, k], gr.at[r, k], y_peers[k])
            for k in range(3)
        ]

    pos_copies = [
        copy(POS.at[y], POS.at[y], gs.at[3, k], gr.at[3, k], y_peers[k]) for k in range(3)
    ]
    for one in state_copies(0) + pos_copies:
        one.start()
    for one in wo_copies(0):
        one.start()

    def pump_prompt(c, carry):
        pump(c, carry)

        @pl.when(ready + c - 1 < 12)
        def _():
            prompt(ready + c - 1)

        return carry

    lax.fori_loop(1, before, pump_prompt, 0)
    lax.fori_loop(jnp.minimum(ready + before - 1, 12), 12, only_prompt, 0)
    loads[8].wait()
    loads[9].wait()
    loads[10].wait()
    for one in state_copies(0) + pos_copies:
        one.wait()

    own_rows = pl.ds(pl.multiple_of(y * 32, 32), 32)
    start_slot = jnp.logical_and(tm == 0, zh == 0)

    def mod(k):
        return MODS[k, 0:1, :]

    def one_round(r, carry):
        halves = XIN[r].astype(F32)
        X = jnp.concatenate(
            [halves[i // 2, :, 64 * (i % 2) : 64 * (i % 2) + 64] for i in range(8)], axis=0
        ).astype(BF16)
        H[...] = nn(X, PATCH[...]) + POS[...].reshape(128, 1536).astype(F32)
        ln_rows(H, N, mod(0), mod(1), 0, 128)

        @pl.when(r == 0)
        def _():
            text_copy.wait()
            for i in range(3):
                at = slice(i * 64, (i + 1) * 64)
                CKN[0, i] = CS[zh, at, :].astype(F32).T.astype(BF16)
                CKN[1, i] = CRECV[at, :].astype(F32).T.astype(BF16)
            CVT[0] = CS[zh, 192:384, :]
            CVT[1] = CRECV[192:384, :]
            lax.fori_loop(1, 4, arrive, 0)

        parts = []

        def head_copies(p):
            at = pl.ds(p * 128, 128)
            return [
                copy(
                    AB.at[r, y, :, at],
                    AB.at[r, y, :, at],
                    ats.at[r, p, k],
                    atr.at[r, p, k],
                    y_peers[k],
                )
                for k in range(3)
            ]

        def send_heads(p):
            AB[r, y, :, p * 128 : (p + 1) * 128] = jnp.concatenate(parts, axis=0).T.astype(BF16)
            for one in head_copies(p):
                one.start()
            parts.clear()

        attended = [head_copies(p) for p in range(3)]
        for s in range(2):
            joint = nt(WB[s, HEADS_AT:UP_AT, :], N[...])
            query = head_norm_t(joint[:192], GAINS[0]).astype(BF16)
            keys = head_norm_t(joint[192:384], GAINS[1])
            values = joint[384:].astype(BF16)
            for i in range(3):
                key_rows = jnp.concatenate([keys[i].T.astype(BF16), CKN[s, i]], axis=0)
                scores = nn(key_rows, query[i]) * 0.125
                powers = jnp.exp(scores)
                probs = (powers / jnp.sum(powers, axis=0, keepdims=True)).astype(BF16)
                both = jnp.concatenate(
                    [values[i * 64 : (i + 1) * 64], CVT[s, i * 64 : (i + 1) * 64, :]], axis=1
                )
                parts.append(nn(both, probs))
                if len(parts) == 2:
                    send_heads((3 * s + i) // 2)

        @pl.when(r == 0)
        def _():
            for one, forward in zip(wo_copies(0), wo_forwards(0)):
                one.wait_recv()
                forward.start()
            lax.fori_loop(before, middle, pump, 0)
            lax.fori_loop(0, 1, arrive, 0)
            fill = pltpu.make_async_copy(
                WB.at[1, pl.ds(WO_AT, 192)], WOF.at[y, 1], local.at[11]
            )
            fill.start()
            for one, forward in zip(wo_copies(1), wo_forwards(1)):
                one.wait_recv()
                forward.start()
            fill.wait()
            for part in range(2):
                for forward in wo_forwards(part):
                    forward.wait_recv()

        def project(k):
            return nn(AB[r, (y + k) % 4], WOF[(y + k) % 4].reshape(384, 1536))

        ACC[...] = project(0)
        for k, i in ((1, 2), (3, 0), (2, 1)):
            for p in range(3):
                attended[p][i].wait_recv()
            ACC[...] += project(k)
        H[...] = H[...] + mod(2) * ACC[...]
        ln_rows(H, N, mod(3), mod(4), 0, 128)

        @pl.when(r == 0)
        def _():
            lax.fori_loop(middle, STEPS, pump, 0)
            lax.fori_loop(4, 8, arrive, 0)

        active = []
        for s in range(2):
            hidden = nn(N[:, 0:768], WB[s, UP_AT:DOWN_AT, 0:768]) + nn(
                N[:, 768:1536], WB[s, UP_AT:DOWN_AT, 768:1536]
            )
            active.append(jax.nn.gelu(hidden, approximate=True).astype(BF16))

        @pl.when(r == 0)
        def _():
            lax.fori_loop(8, CHUNKS, arrive, 0)

        summed = []
        for p in range(2):
            at = slice(p * 768, (p + 1) * 768)
            total = nn(active[0], WB[0, DOWN_AT:ALL_ROWS, at]) + nn(
                active[1], WB[1, DOWN_AT:ALL_ROWS, at]
            )
            ACC[:, at] = total
            RSS[:, at] = total.astype(BF16)
            for k in range(3):
                one = copy(
                    RSS.at[
                        pl.ds(pl.multiple_of(((y + k + 1) % 4) * 32, 32), 32),
                        pl.ds(p * 768, 768),
                    ],
                    RSB.at[r, k, :, pl.ds(p * 768, 768)],
                    rss.at[r, p, k],
                    rsr.at[r, p, k],
                    y_peers[k],
                )
                one.start()
                summed.append(one)
        for one in summed:
            one.wait_recv()
        contract = ACC[own_rows, :]
        for k in range(3):
            contract = contract + RSB[r, k].astype(F32)
        state = ln_mod(H[own_rows, :] + mod(5) * contract, mod(8), mod(9))
        term = step * nt(state, FINAL[...])
        term = jnp.concatenate([term[0:16], term[16:32]], axis=1)
        anchor = jnp.concatenate([XR[0], XR[1]], axis=1)
        term = term - jnp.where(start_slot, anchor, jnp.zeros_like(anchor))

        TZ[r, z] = term
        along_z = [
            copy(TZ.at[r, z], TZ.at[r, z], szs.at[r, k - 1], szr.at[r, k - 1], z_peers[k - 1])
            for k in (4, 3, 5, 2, 6, 1, 7)
        ]
        for one in along_z:
            one.start()
        for one in along_z:
            one.wait_recv()
        lower = TZ[r, zl]
        both_halves = lower + TZ[r, zl + 4]
        below = jnp.zeros_like(term)
        for i in range(8):
            block = TZ[r, i]
            below = below + jnp.where(i % 4 < zl, block, jnp.zeros_like(block))
        SUMS[r, 0] = below
        SUMS[r, 1] = below + both_halves
        XS[r, x, core] = below
        along_x = []
        for k in range(1, 8):
            to_x, to_core = (x + k // 2) % 4, (core + k) % 2
            later = (2 * to_x + to_core > 2 * x + core).astype(jnp.int32)
            one = copy(
                SUMS.at[r, later],
                XS.at[r, x, core],
                sxs.at[r, k - 1],
                sxr.at[r, k - 1],
                device(z, to_x, to_core, y),
            )
            one.start()
            along_x.append(one)
        for one in along_x:
            one.wait_recv()
        base = jnp.zeros_like(term)
        for i in range(8):
            base = base + XS[r, i // 2, i % 2]
        upper = zh == 1

        @pl.when(r < ROUNDS - 1)
        def _():
            earlier = base + jnp.where(upper, lower, jnp.zeros_like(lower))
            XIN[r + 1, y] = jnp.where(start_slot, anchor, -earlier).astype(BF16)
            for one in state_copies(r + 1):
                one.start()
            for one in state_copies(r + 1):
                one.wait()

        @pl.when(r == ROUNDS - 1)
        def _():
            for s, total in enumerate([base + lower, base + both_halves]):
                out[s] = -jnp.where(upper, total[:, 64:128], total[:, 0:64])

        for one in sum(attended, []) + summed + along_x + along_z:
            one.wait_send()
        return carry

    lax.fori_loop(0, ROUNDS, one_round, 0)

    def drain(c, carry):
        z_copy(c).wait_send()
        x_copy(c).wait_send()
        core_copy(c).wait_send()
        return carry

    lax.fori_loop(0, CHUNKS, drain, 0)
    for part in range(2):
        for one in wo_copies(part) + wo_forwards(part):
            one.wait_send()


def per_device(
    trajectory,
    window_start,
    step_sizes,
    modulation,
    context,
    position_embed,
    patch_weight,
    heads_weight,
    query_gain,
    key_gain,
    text_weight,
    output_weight,
    up_weight,
    down_weight,
    final_weight,
):
    heads = heads_weight.transpose(1, 2, 0).reshape(HEAD_ROWS, 1536)
    text = text_weight.transpose(1, 2, 0).reshape(384, 1536)
    vmem = pl.BlockSpec(memory_space=pltpu.VMEM)
    hbm = pl.BlockSpec(memory_space=pl.ANY)
    dma = pltpu.SemaphoreType.DMA
    R = ROUNDS
    return pl.pallas_call(
        kernel,
        out_shape=jax.ShapeDtypeStruct((2, 16, 64), F32),
        in_specs=[vmem, pl.BlockSpec(memory_space=pltpu.SMEM), vmem, hbm, hbm, vmem, hbm, hbm]
        + [vmem, vmem, hbm, hbm, hbm, hbm, hbm],
        out_specs=vmem,
        scratch_shapes=[
            pltpu.VMEM((2, ALL_ROWS, 1536), BF16),
            pltpu.VMEM((4, 2, 192, 1536), BF16),
            pltpu.VMEM((384, 1536), BF16),
            pltpu.VMEM((4, 32, 1536), BF16),
            pltpu.VMEM((R, 4, 16, 128), BF16),
            pltpu.VMEM((2, 16, 64), F32),
            pltpu.VMEM((128, 1536), BF16),
            pltpu.VMEM((2, 3, 128, 64), BF16),
            pltpu.VMEM((2, 192, 128), BF16),
            pltpu.VMEM((2, 384, 128), BF16),
            pltpu.VMEM((384, 128), BF16),
            pltpu.VMEM((128, 1536), F32),
            pltpu.VMEM((128, 1536), BF16),
            pltpu.VMEM((128, 1536), F32),
            pltpu.VMEM((R, 4, 128, 384), BF16),
            pltpu.VMEM((128, 1536), BF16),
            pltpu.VMEM((R, 3, 32, 1536), BF16),
            pltpu.VMEM((R, 8, 16, 128), F32),
            pltpu.VMEM((R, 2, 16, 128), F32),
            pltpu.VMEM((R, 4, 2, 16, 128), F32),
            pltpu.VMEM((10, 112, 1536), BF16),
            pltpu.VMEM((10, 8, 1536), F32),
            pltpu.VMEM((128, 1536), BF16),
            pltpu.VMEM((64, 1536), BF16),
            pltpu.VMEM((64, 1536), BF16),
            pltpu.VMEM((2, 64, 128), F32),
            dma((12,)),
            dma((CHUNKS,)),
            dma((CHUNKS,)),
            dma((CHUNKS,)),
            dma((CHUNKS,)),
            dma((CHUNKS,)),
            dma((CHUNKS,)),
            dma((2, 3)),
            dma((2, 3)),
            dma((2, 3)),
            dma((2, 3)),
            dma((2,)),
            dma((2,)),
            dma((4, 3)),
            dma((4, 3)),
            dma,
            dma,
            dma((R, 3, 3)),
            dma((R, 3, 3)),
            dma((R, 2, 3)),
            dma((R, 2, 3)),
            dma((R, 7)),
            dma((R, 7)),
            dma((R, 7)),
            dma((R, 7)),
        ],
        compiler_params=pltpu.CompilerParams(
            collective_id=0, has_side_effects=True, vmem_limit_bytes=56 << 20
        ),
        cost_estimate=pl.CostEstimate(
            flops=7_000_000_000, bytes_accessed=10_000_000, transcendentals=1_000_000
        ),
        name="picard",
    )(
        trajectory,
        window_start,
        step_sizes[None],
        modulation.transpose(1, 0, 2),
        context,
        position_embed,
        patch_weight,
        heads,
        query_gain[None],
        key_gain[None],
        text,
        output_weight,
        up_weight,
        down_weight,
        final_weight.T,
    )


def solution(mesh):
    return jax.shard_map(
        per_device,
        mesh=mesh,
        in_specs=(
            P("tm", "tp", None),
            P(),
            P(),
            P(),
            P(),
            P("tp", None),
            P(),
            P(None, None, "tp"),
            P(),
            P(),
            P(None, None, "tp"),
            P("tp", None),
            P(None, "tp"),
            P("tp", None),
            P(),
        ),
        out_specs=P("tm", "tp", None),
        check_vma=False,
    )
```

```python
import functools

import jax
import jax.numpy as jnp
from jax import lax
from jax.experimental import pallas as pl
from jax.experimental.pallas import tpu as pltpu
from jax.sharding import PartitionSpec as P

ROUNDS = 3
EPSILON = 1e-06
MESH = pl.DeviceIdType.MESH
F32 = jnp.float32
BF16 = jnp.bfloat16

LAG = 3
CHUNKS = 18
CHUNK = 128
STEPS = CHUNKS + LAG
PIECE = 32
HEAD_ROWS = 576
FAR_FIRST = (1, 0, 2)
FIRST = 6
HEADS_AT, WO_AT, UP_AT, DOWN_AT, ALL_ROWS = 0, 576, 768, 1536, 2304


def nt(a, b):
    return lax.dot_general(a, b, (((1,), (1,)), ((), ())), preferred_element_type=F32)


def nn(a, b):
    return jnp.dot(a, b, preferred_element_type=F32)


def ln_mod(values, shift, scale):
    average = jnp.mean(values, axis=-1, keepdims=True)
    centered = values - average
    spread = jnp.mean(centered * centered, axis=-1, keepdims=True)
    return (centered * lax.rsqrt(spread + EPSILON) * (1.0 + scale) + shift).astype(BF16)


def ln_rows(source, target, shift, scale, start, rows):
    def block(i, carry):
        at = pl.ds(pl.multiple_of(start + i * 16, 16), 16)
        target[at, :] = ln_mod(source[at, :].astype(F32), shift, scale)
        return carry

    lax.fori_loop(0, rows // 16, block, 0, unroll=8 if rows == 128 else 2)


def head_norm_t(values, gain):
    split = values.reshape(values.shape[0] // 64, 64, values.shape[1])
    square = jnp.mean(split * split, axis=1, keepdims=True)
    return split * lax.rsqrt(square + EPSILON) * gain[None]


def device(z, x, core, y):
    z, x, y = (z + 8) % 8, (x + 4) % 4, (y + 4) % 4
    return (((z % 4) * 4 + x) * 2 + core, y * 2 + z // 4)


def kernel(
    traj, start, steps, table, ctx, pos, patch, heads, q_gain, k_gain, text, wo, up, down, final,
    out,
    WB, WOF, TT, POS, XIN, XR, TN, CKN, CVT, CS, CRECV, H, N, ACC, AB, RSS, RSB,
    TZ, SUMS, XS, TABLE, MODS, CTX, PATCH, FINAL, GAINS,
    local, zs, zr, xs, xr, cs, cr, wos, wor, wfs, wfr,
    exs, exr, gs, gr, txs, txr, ats, atr, rss, rsr, sxs, sxr, szs, szr, mxs, mxr,
):
    tm, tp = lax.axis_index("tm"), lax.axis_index("tp")
    zl, x, core = tm // 8, (tm // 2) % 4, tm % 2
    y, zh = tp // 2, tp % 2
    z = zh * 4 + zl
    way = 1 - 2 * core

    def copy(src, dst, send, recv, to):
        return pltpu.make_async_remote_copy(
            src_ref=src, dst_ref=dst, send_sem=send, recv_sem=recv, device_id=to, device_id_type=MESH
        )

    y_peers = [device(z, x, core, y + k) for k in (1, 2, 3)]
    z_peers = [device(z + k, x, core, y) for k in range(1, 8)]
    other_core = device(z, x, 1 - core, y)
    other_half = device(z + 4, x, core, y)

    barrier = pltpu.get_barrier_semaphore()
    x_peers = [device(z, x + k // 2, (core + k) % 2, y) for k in range(1, 8)]
    everyone = y_peers + x_peers + z_peers
    for peer in everyone:
        pl.semaphore_signal(barrier, inc=1, device_id=peer, device_id_type=MESH)

    loads = [
        pltpu.make_async_copy(src, dst, local.at[i])
        for i, (src, dst) in enumerate(
            [
                (wo, WB.at[0, pl.ds(WO_AT, 192)]),
                (heads, WB.at[0, pl.ds(HEADS_AT, HEAD_ROWS)]),
                (up.at[pl.ds(0, 768)], WB.at[0, pl.ds(UP_AT, 768), pl.ds(0, 768)]),
                (up.at[pl.ds(768, 768)], WB.at[0, pl.ds(UP_AT, 768), pl.ds(768, 768)]),
                (down, WB.at[0, pl.ds(DOWN_AT, 768)]),
                (table, TABLE),
                (ctx, CTX),
                (text, TT),
                (patch, PATCH),
                (wo, WOF.at[y, 0]),
                (final, FINAL),
            ]
        )
    ]
    for i in (1, 0, 5, 6, 7, 2, 3, 4, 8, 9, 10):
        loads[i].start()

    pl.semaphore_wait(barrier, len(everyone))

    half = pl.ds(pl.multiple_of(zh * 16, 16), 16)
    ex_x = copy(traj.at[1 - zh], XR.at[zh], exs.at[0], exr.at[0], other_half)
    ex_pos = copy(pos, POS.at[y, half], exs.at[1], exr.at[1], other_half)
    ex_x.start()
    ex_pos.start()
    XR[zh] = traj[zh]
    POS[y, half, :] = pos[...]

    even = x % 2
    first = jnp.where(core == 0, zl == 3, zl == 0)
    own = 1 - first.astype(jnp.int32)
    z_quarter = 2 * core + even

    def rows(quarter, c):
        return pl.ds(pl.multiple_of(c * CHUNK + quarter * PIECE, 16), PIECE)

    def z_copy(c):
        at = rows(z_quarter, c)
        return copy(
            WB.at[own, at], WB.at[1, at], zs.at[c], zr.at[c], device(z + way, x, core, y)
        )

    def x_copy(c):
        at = rows(z_quarter, c)
        return copy(WB.at[1, at], WB.at[1, at], xs.at[c], xr.at[c], device(z, x + way, core, y))

    def core_copy(c):
        at = pl.ds(pl.multiple_of(c * CHUNK + core * 2 * PIECE, 16), 2 * PIECE)
        return copy(WB.at[1, at], WB.at[1, at], cs.at[c], cr.at[c], other_core)

    def send_own(low, high):
        @pl.when(first)
        def _():
            def send(c, carry):
                z_copy(c).start()
                return carry

            lax.fori_loop(low, high, send, 0)

    loads[1].wait()
    loads[0].wait()
    send_own(0, FIRST)

    entry = start[0] + tm * 2
    line = lax.broadcasted_iota(jnp.int32, (8, 112), 0)
    wanted = entry + jnp.where(line == 0, zh, 1 - zh)
    pick = (lax.broadcasted_iota(jnp.int32, (8, 112), 1) == wanted).astype(F32)
    step = jnp.sum(pick[0:1] * steps[...], axis=1, keepdims=True)
    pick = pick.astype(BF16)
    loads[5].wait()
    for k in range(10):
        MODS[k] = nn(pick, TABLE[k])
    GAINS[0] = jnp.broadcast_to(q_gain[...], (128, 64)).T
    GAINS[1] = jnp.broadcast_to(k_gain[...], (128, 64)).T

    loads[2].wait()
    loads[3].wait()
    loads[4].wait()
    send_own(FIRST, CHUNKS)

    def pump_x(c):
        x_copy(c).wait_recv()
        core_copy(c).start()

    def pump(c, carry):
        @pl.when(c < CHUNKS)
        def _():
            z_copy(c).wait_recv()

            @pl.when(jnp.logical_not(first))
            def _():
                z_copy(c).start()

            x_copy(c).start()

        @pl.when(c >= LAG)
        def _():
            pump_x(c - LAG)

        return carry

    def arrive(c, carry):
        core_copy(c).wait_recv()
        return carry

    mine = pl.ds(pl.multiple_of(core * 96, 16), 96)

    def wo_copy(part, k):
        return copy(
            WB.at[part, pl.ds(pl.multiple_of(WO_AT + core * 96, 16), 96)],
            WOF.at[y, part, mine],
            wos.at[part, k],
            wor.at[part, k],
            y_peers[k],
        )

    def wo_forward(part, k):
        at = WOF.at[(y + 3 - k) % 4, part, mine]
        return copy(at, at, wfs.at[part, k], wfr.at[part, k], other_core)

    def wo_copies(part):
        return [wo_copy(part, k) for k in range(3)]

    def wo_forwards(part):
        return [wo_forward(part, k) for k in range(3)]

    loads[6].wait()
    loads[7].wait()
    text_copy = copy(CS.at[1 - zh], CRECV, txs, txr, other_half)

    def prompt(c):
        of_other = c < 6
        slot = jnp.where(of_other, 1 - zh, zh)
        part = c % 6

        @pl.when(part < 4)
        def _():
            shift, scale = (
                jnp.where(of_other, MODS[k, 1:2, :], MODS[k, 0:1, :]) for k in (6, 7)
            )
            ln_rows(CTX, TN, shift, scale, part * 32, 32)

        @pl.when(part == 4)
        def _():
            keys = head_norm_t(nt(TT[0:192, :], TN[...]), GAINS[1])
            CS[slot, 0:192, :] = keys.reshape(192, 128).astype(BF16)

        @pl.when(part == 5)
        def _():
            CS[slot, 192:384, :] = nt(TT[192:384, :], TN[...]).astype(BF16)

        @pl.when(c == 5)
        def _():
            text_copy.start()

    def only_prompt(c, carry):
        prompt(c)
        return carry

    hop = jnp.where(core == 0, zl + 1, 4 - zl)

    def by_hop(*values):
        return jnp.where(
            hop == 1,
            values[0],
            jnp.where(hop == 2, values[1], jnp.where(hop == 3, values[2], values[3])),
        )

    ready = by_hop(6, 6, 12, 12)
    before, between, middle = by_hop(18, 16, 13, 10), by_hop(18, 18, 15, 11), by_hop(21, 21, 21, 16)
    lax.fori_loop(0, ready, only_prompt, 0)
    pump(0, 0)

    ex_x.wait()
    ex_pos.wait()
    anchor = jnp.concatenate([XR[0], XR[1]], axis=1)
    XIN[0, y] = anchor.astype(BF16)

    def state_copies(r):
        return [
            copy(XIN.at[r, y], XIN.at[r, y], gs.at[r, k], gr.at[r, k], y_peers[k])
            for k in FAR_FIRST
        ]

    pos_copies = [
        copy(POS.at[y], POS.at[y], gs.at[3, k], gr.at[3, k], y_peers[k]) for k in range(3)
    ]
    for one in state_copies(0) + pos_copies:
        one.start()
    def pump_prompt(c, carry):
        pump(c, carry)

        @pl.when(ready + c - 1 < 12)
        def _():
            prompt(ready + c - 1)

        return carry

    lax.fori_loop(1, 4, pump_prompt, 0)
    for one in wo_copies(0):
        one.start()
    lax.fori_loop(4, before, pump_prompt, 0)
    loads[8].wait()
    loads[9].wait()
    loads[10].wait()
    for one in state_copies(0) + pos_copies:
        one.wait()

    own_rows = pl.ds(pl.multiple_of(y * 32, 32), 32)
    their_rows = [
        pl.ds(pl.multiple_of(((y + k + 1) % 4) * 32, 32), 32) for k in range(3)
    ]
    start_slot = jnp.logical_and(tm == 0, zh == 0)

    def mod(k):
        return MODS[k, 0:1, :]

    def one_round(r, carry):
        halves = XIN[r].astype(F32)
        X = jnp.concatenate(
            [halves[i // 2, :, 64 * (i % 2) : 64 * (i % 2) + 64] for i in range(8)], axis=0
        ).astype(BF16)
        H[...] = nn(X, PATCH[...]) + POS[...].reshape(128, 1536).astype(F32)
        ln_rows(H, N, mod(0), mod(1), 0, 128)

        @pl.when(r == 0)
        def _():
            text_copy.wait()
            for i in range(3):
                at = slice(i * 64, (i + 1) * 64)
                CKN[0, i] = CS[zh, at, :].astype(F32).T.astype(BF16)
                CKN[1, i] = CRECV[at, :].astype(F32).T.astype(BF16)
            CVT[0] = CS[zh, 192:384, :]
            CVT[1] = CRECV[192:384, :]
            lax.fori_loop(0, FIRST, arrive, 0)
            for k in (0, 2):
                wo_copy(1, k).start()

        parts = []

        def head_copies(p):
            at = pl.ds(p * 128, 128)
            return [
                copy(
                    AB.at[r, y, :, at],
                    AB.at[r, y, :, at],
                    ats.at[r, p, k],
                    atr.at[r, p, k],
                    y_peers[k],
                )
                for k in FAR_FIRST
            ]

        def send_heads(p):
            AB[r, y, :, p * 128 : (p + 1) * 128] = jnp.concatenate(parts, axis=0).T.astype(BF16)
            parts.clear()

            @pl.when(r > 0)
            def _():
                for one in head_copies(p):
                    one.start()

        attended = [head_copies(p) for p in range(3)]
        for s in range(2):
            if s == 1:

                @pl.when(r == 0)
                def _():
                    lax.fori_loop(before, between, pump, 0)

            joint = nt(WB[s, HEADS_AT:WO_AT, :], N[...])
            query = head_norm_t(joint[:192], GAINS[0]).astype(BF16)
            keys = head_norm_t(joint[192:384], GAINS[1])
            values = joint[384:].astype(BF16)
            for i in range(3):
                key_rows = jnp.concatenate([keys[i].T.astype(BF16), CKN[s, i]], axis=0)
                scores = nn(key_rows, query[i]) * 0.125
                powers = jnp.exp(scores)
                probs = (powers / jnp.sum(powers, axis=0, keepdims=True)).astype(BF16)
                both = jnp.concatenate(
                    [values[i * 64 : (i + 1) * 64], CVT[s, i * 64 : (i + 1) * 64, :]], axis=1
                )
                parts.append(nn(both, probs))
                if len(parts) == 2:
                    send_heads((3 * s + i) // 2)

        @pl.when(r == 0)
        def _():
            ACC[...] = nn(AB[r, y, :, 0:192], WB[0, WO_AT:UP_AT, :]) + nn(
                AB[r, y, :, 192:384], WB[1, WO_AT:UP_AT, :]
            )
            RSS[1] = ACC[...].astype(BF16)
            mixed = [
                copy(RSS.at[1, their_rows[k]], RSB.at[3, k], mxs.at[0, k], mxr.at[0, k], y_peers[k])
                for k in FAR_FIRST
            ]
            for one in mixed:
                one.start()
            lax.fori_loop(between, middle, pump, 0)
            for one in mixed:
                one.wait_recv()
            total = ACC[own_rows, :]
            for k in range(3):
                total = total + RSB[3, k].astype(F32)
            H[own_rows, :] = H[own_rows, :] + mod(2) * total
            ln_rows(H, N, mod(3), mod(4), y * 32, 32)
            normed = [
                copy(N.at[own_rows], N.at[own_rows], mxs.at[1, k], mxr.at[1, k], y_peers[k])
                for k in FAR_FIRST
            ]
            for one in normed:
                one.start()
            lax.fori_loop(middle, STEPS, pump, 0)
            for part, k in ((0, 0), (0, 2), (0, 1), (1, 0), (1, 2)):
                wo_copy(part, k).wait_recv()
                wo_forward(part, k).start()
            fill = pltpu.make_async_copy(
                WB.at[1, pl.ds(WO_AT, 192)], WOF.at[y, 1], local.at[11]
            )
            fill.start()
            lax.fori_loop(FIRST, CHUNKS, arrive, 0)
            fill.wait()
            for one in normed:
                one.wait_recv()
            for one in mixed + normed:
                one.wait_send()

        @pl.when(r == 1)
        def _():
            wo_copy(1, 1).wait_recv()
            wo_forward(1, 1).start()
            for part in range(2):
                for forward in wo_forwards(part):
                    forward.wait_recv()

        def project(k):
            return nn(AB[r, (y + k) % 4], WOF[(y + k) % 4].reshape(384, 1536))

        @pl.when(r > 0)
        def _():
            ACC[...] = project(0)
            for k, i in ((1, 2), (3, 1), (2, 0)):
                for p in range(3):
                    attended[p][i].wait_recv()
                ACC[...] += project(k)
            H[...] = H[...] + mod(2) * ACC[...]
            ln_rows(H, N, mod(3), mod(4), 0, 128)

        active = []
        for s in range(2):
            hidden = nn(N[:, 0:768], WB[s, UP_AT:DOWN_AT, 0:768]) + nn(
                N[:, 768:1536], WB[s, UP_AT:DOWN_AT, 768:1536]
            )
            active.append(jax.nn.gelu(hidden, approximate=True).astype(BF16))

        summed = []
        for p in range(2):
            at = slice(p * 768, (p + 1) * 768)
            total = nn(active[0], WB[0, DOWN_AT:ALL_ROWS, at]) + nn(
                active[1], WB[1, DOWN_AT:ALL_ROWS, at]
            )
            ACC[:, at] = total
            RSS[0, :, at] = total.astype(BF16)
            for k in FAR_FIRST:
                one = copy(
                    RSS.at[0, their_rows[k], pl.ds(p * 768, 768)],
                    RSB.at[r, k, :, pl.ds(p * 768, 768)],
                    rss.at[r, p, k],
                    rsr.at[r, p, k],
                    y_peers[k],
                )
                one.start()
                summed.append(one)
        for one in summed:
            one.wait_recv()

        @pl.when(r == 0)
        def _():
            wo_copy(1, 1).start()

        contract = ACC[own_rows, :]
        for k in range(3):
            contract = contract + RSB[r, k].astype(F32)
        state = ln_mod(H[own_rows, :] + mod(5) * contract, mod(8), mod(9))
        term = step * nt(state, FINAL[...])
        term = jnp.concatenate([term[0:16], term[16:32]], axis=1)
        anchor = jnp.concatenate([XR[0], XR[1]], axis=1)
        term = term - jnp.where(start_slot, anchor, jnp.zeros_like(anchor))

        TZ[r, z] = term
        along_z = [
            copy(TZ.at[r, z], TZ.at[r, z], szs.at[r, k - 1], szr.at[r, k - 1], z_peers[k - 1])
            for k in (4, 3, 5, 2, 6, 1, 7)
        ]
        for one in along_z:
            one.start()
        for one in along_z:
            one.wait_recv()
        lower = TZ[r, zl]
        both_halves = lower + TZ[r, zl + 4]
        below = jnp.zeros_like(term)
        for i in range(8):
            block = TZ[r, i]
            below = below + jnp.where(i % 4 < zl, block, jnp.zeros_like(block))
        SUMS[r, 0] = below
        SUMS[r, 1] = below + both_halves
        XS[r, x, core] = below
        along_x = []
        for k in (4, 5, 2, 3, 6, 7, 1):
            to_x, to_core = (x + k // 2) % 4, (core + k) % 2
            later = (2 * to_x + to_core > 2 * x + core).astype(jnp.int32)
            one = copy(
                SUMS.at[r, later],
                XS.at[r, x, core],
                sxs.at[r, k - 1],
                sxr.at[r, k - 1],
                device(z, to_x, to_core, y),
            )
            one.start()
            along_x.append(one)
        for one in along_x:
            one.wait_recv()
        base = jnp.zeros_like(term)
        for i in range(8):
            base = base + XS[r, i // 2, i % 2]
        upper = zh == 1

        @pl.when(r < ROUNDS - 1)
        def _():
            earlier = base + jnp.where(upper, lower, jnp.zeros_like(lower))
            XIN[r + 1, y] = jnp.where(start_slot, anchor, -earlier).astype(BF16)
            for one in state_copies(r + 1):
                one.start()
            for one in state_copies(r + 1):
                one.wait()

        @pl.when(r == ROUNDS - 1)
        def _():
            for s, total in enumerate([base + lower, base + both_halves]):
                out[s] = -jnp.where(upper, total[:, 64:128], total[:, 0:64])

        for one in summed + along_x + along_z:
            one.wait_send()

        @pl.when(r > 0)
        def _():
            for one in sum(attended, []):
                one.wait_send()

        return carry

    lax.fori_loop(0, ROUNDS, one_round, 0)

    def drain(c, carry):
        z_copy(c).wait_send()
        x_copy(c).wait_send()
        core_copy(c).wait_send()
        return carry

    lax.fori_loop(0, CHUNKS, drain, 0)
    for part in range(2):
        for one in wo_copies(part) + wo_forwards(part):
            one.wait_send()


def per_device(
    trajectory,
    window_start,
    step_sizes,
    modulation,
    context,
    position_embed,
    patch_weight,
    heads_weight,
    query_gain,
    key_gain,
    text_weight,
    output_weight,
    up_weight,
    down_weight,
    final_weight,
):
    heads = heads_weight.transpose(1, 2, 0).reshape(HEAD_ROWS, 1536)
    text = text_weight.transpose(1, 2, 0).reshape(384, 1536)
    vmem = pl.BlockSpec(memory_space=pltpu.VMEM)
    hbm = pl.BlockSpec(memory_space=pl.ANY)
    dma = pltpu.SemaphoreType.DMA
    R = ROUNDS
    return pl.pallas_call(
        kernel,
        out_shape=jax.ShapeDtypeStruct((2, 16, 64), F32),
        in_specs=[vmem, pl.BlockSpec(memory_space=pltpu.SMEM), vmem, hbm, hbm, vmem, hbm, hbm]
        + [vmem, vmem, hbm, hbm, hbm, hbm, hbm],
        out_specs=vmem,
        scratch_shapes=[
            pltpu.VMEM((2, ALL_ROWS, 1536), BF16),
            pltpu.VMEM((4, 2, 192, 1536), BF16),
            pltpu.VMEM((384, 1536), BF16),
            pltpu.VMEM((4, 32, 1536), BF16),
            pltpu.VMEM((R, 4, 16, 128), BF16),
            pltpu.VMEM((2, 16, 64), F32),
            pltpu.VMEM((128, 1536), BF16),
            pltpu.VMEM((2, 3, 128, 64), BF16),
            pltpu.VMEM((2, 192, 128), BF16),
            pltpu.VMEM((2, 384, 128), BF16),
            pltpu.VMEM((384, 128), BF16),
            pltpu.VMEM((128, 1536), F32),
            pltpu.VMEM((128, 1536), BF16),
            pltpu.VMEM((128, 1536), F32),
            pltpu.VMEM((R, 4, 128, 384), BF16),
            pltpu.VMEM((2, 128, 1536), BF16),
            pltpu.VMEM((R + 1, 3, 32, 1536), BF16),
            pltpu.VMEM((R, 8, 16, 128), F32),
            pltpu.VMEM((R, 2, 16, 128), F32),
            pltpu.VMEM((R, 4, 2, 16, 128), F32),
            pltpu.VMEM((10, 112, 1536), BF16),
            pltpu.VMEM((10, 8, 1536), F32),
            pltpu.VMEM((128, 1536), BF16),
            pltpu.VMEM((64, 1536), BF16),
            pltpu.VMEM((64, 1536), BF16),
            pltpu.VMEM((2, 64, 128), F32),
            dma((12,)),
            dma((CHUNKS,)),
            dma((CHUNKS,)),
            dma((CHUNKS,)),
            dma((CHUNKS,)),
            dma((CHUNKS,)),
            dma((CHUNKS,)),
            dma((2, 3)),
            dma((2, 3)),
            dma((2, 3)),
            dma((2, 3)),
            dma((2,)),
            dma((2,)),
            dma((4, 3)),
            dma((4, 3)),
            dma,
            dma,
            dma((R, 3, 3)),
            dma((R, 3, 3)),
            dma((R, 2, 3)),
            dma((R, 2, 3)),
            dma((R, 7)),
            dma((R, 7)),
            dma((R, 7)),
            dma((R, 7)),
            dma((2, 3)),
            dma((2, 3)),
        ],
        compiler_params=pltpu.CompilerParams(
            collective_id=0, has_side_effects=True, vmem_limit_bytes=56 << 20
        ),
        cost_estimate=pl.CostEstimate(
            flops=7_000_000_000, bytes_accessed=10_000_000, transcendentals=1_000_000
        ),
        name="picard",
    )(
        trajectory,
        window_start,
        step_sizes[None],
        modulation.transpose(1, 0, 2),
        context,
        position_embed,
        patch_weight,
        heads,
        query_gain[None],
        key_gain[None],
        text,
        output_weight,
        up_weight,
        down_weight,
        final_weight.T,
    )


def solution(mesh):
    return jax.shard_map(
        per_device,
        mesh=mesh,
        in_specs=(
            P("tm", "tp", None),
            P(),
            P(),
            P(),
            P(),
            P("tp", None),
            P(),
            P(None, None, "tp"),
            P(),
            P(),
            P(None, None, "tp"),
            P("tp", None),
            P(None, "tp"),
            P("tp", None),
            P(),
        ),
        out_specs=P("tm", "tp", None),
        check_vma=False,
    )
```

```python
import functools

import jax
import jax.numpy as jnp
from jax import lax
from jax.experimental import pallas as pl
from jax.experimental.pallas import tpu as pltpu
from jax.sharding import PartitionSpec as P

ROUNDS = 3
EPSILON = 1e-06
MESH = pl.DeviceIdType.MESH
F32 = jnp.float32
BF16 = jnp.bfloat16

LAG = 4
CHUNKS = 18
CHUNK = 128
STEPS = CHUNKS + LAG
PIECE = 32
HEAD_ROWS = 576
FAR_FIRST = (1, 0, 2)
FIRST = 6
HEADS_AT, WO_AT, UP_AT, DOWN_AT, ALL_ROWS = 0, 576, 768, 1536, 2304


def nt(a, b):
    return lax.dot_general(a, b, (((1,), (1,)), ((), ())), preferred_element_type=F32)


def nn(a, b):
    return jnp.dot(a, b, preferred_element_type=F32)


def ln_mod(values, shift, scale):
    average = jnp.mean(values, axis=-1, keepdims=True)
    centered = values - average
    spread = jnp.mean(centered * centered, axis=-1, keepdims=True)
    return (centered * lax.rsqrt(spread + EPSILON) * (1.0 + scale) + shift).astype(BF16)


def ln_rows(source, target, shift, scale, start, rows):
    def block(i, carry):
        at = pl.ds(pl.multiple_of(start + i * 16, 16), 16)
        target[at, :] = ln_mod(source[at, :].astype(F32), shift, scale)
        return carry

    lax.fori_loop(0, rows // 16, block, 0, unroll=8 if rows == 128 else 2)


def head_norm_t(values, gain):
    split = values.reshape(values.shape[0] // 64, 64, values.shape[1])
    square = jnp.mean(split * split, axis=1, keepdims=True)
    return split * lax.rsqrt(square + EPSILON) * gain[None]


def device(z, x, core, y):
    z, x, y = (z + 8) % 8, (x + 4) % 4, (y + 4) % 4
    return (((z % 4) * 4 + x) * 2 + core, y * 2 + z // 4)


def kernel(
    traj, start, steps, table, ctx, pos, patch, heads, q_gain, k_gain, text, wo, up, down, final,
    out,
    WB, WOF, TT, POS, XIN, XR, TN, CKN, CVT, CS, CRECV, H, N, ACC, AB, RSS, RSB,
    TZ, SUMS, XS, TABLE, MODS, CTX, PATCH, FINAL, GAINS,
    local, zs, zr, xs, xr, cs, cr, wos, wor, wfs, wfr,
    exs, exr, gs, gr, txs, txr, ats, atr, rss, rsr, sxs, sxr, szs, szr, mxs, mxr,
):
    tm, tp = lax.axis_index("tm"), lax.axis_index("tp")
    zl, x, core = tm // 8, (tm // 2) % 4, tm % 2
    y, zh = tp // 2, tp % 2
    z = zh * 4 + zl
    way = 1 - 2 * core

    def copy(src, dst, send, recv, to):
        return pltpu.make_async_remote_copy(
            src_ref=src, dst_ref=dst, send_sem=send, recv_sem=recv, device_id=to, device_id_type=MESH
        )

    y_peers = [device(z, x, core, y + k) for k in (1, 2, 3)]
    z_peers = [device(z + k, x, core, y) for k in range(1, 8)]
    other_core = device(z, x, 1 - core, y)
    other_half = device(z + 4, x, core, y)

    barrier = pltpu.get_barrier_semaphore()
    x_peers = [device(z, x + k // 2, (core + k) % 2, y) for k in range(1, 8)]
    everyone = y_peers + x_peers + z_peers
    for peer in everyone:
        pl.semaphore_signal(barrier, inc=1, device_id=peer, device_id_type=MESH)

    loads = [
        pltpu.make_async_copy(src, dst, local.at[i])
        for i, (src, dst) in enumerate(
            [
                (wo, WB.at[0, pl.ds(WO_AT, 192)]),
                (heads, WB.at[0, pl.ds(HEADS_AT, HEAD_ROWS)]),
                (up.at[pl.ds(0, 768)], WB.at[0, pl.ds(UP_AT, 768), pl.ds(0, 768)]),
                (up.at[pl.ds(768, 768)], WB.at[0, pl.ds(UP_AT, 768), pl.ds(768, 768)]),
                (down, WB.at[0, pl.ds(DOWN_AT, 768)]),
                (table, TABLE),
                (ctx, CTX),
                (text, TT),
                (patch, PATCH),
                (wo, WOF.at[y, 0]),
                (final, FINAL),
            ]
        )
    ]
    for i in (1, 0, 5, 6, 7, 2, 3, 4, 8, 9, 10):
        loads[i].start()

    pl.semaphore_wait(barrier, len(everyone))

    half = pl.ds(pl.multiple_of(zh * 16, 16), 16)
    ex_x = copy(traj.at[1 - zh], XR.at[zh], exs.at[0], exr.at[0], other_half)
    ex_pos = copy(pos, POS.at[y, half], exs.at[1], exr.at[1], other_half)
    ex_x.start()
    ex_pos.start()
    XR[zh] = traj[zh]
    POS[y, half, :] = pos[...]

    even = x % 2
    first = jnp.where(core == 0, zl == 3, zl == 0)
    own = 1 - first.astype(jnp.int32)
    z_quarter = 2 * core + even

    def rows(quarter, c):
        return pl.ds(pl.multiple_of(c * CHUNK + quarter * PIECE, 16), PIECE)

    def z_copy(c):
        at = rows(z_quarter, c)
        return copy(
            WB.at[own, at], WB.at[1, at], zs.at[c], zr.at[c], device(z + way, x, core, y)
        )

    def x_copy(c):
        at = rows(z_quarter, c)
        return copy(WB.at[1, at], WB.at[1, at], xs.at[c], xr.at[c], device(z, x + way, core, y))

    def core_copy(c):
        at = pl.ds(pl.multiple_of(c * CHUNK + core * 2 * PIECE, 16), 2 * PIECE)
        return copy(WB.at[1, at], WB.at[1, at], cs.at[c], cr.at[c], other_core)

    def send_own(low, high):
        @pl.when(first)
        def _():
            def send(c, carry):
                z_copy(c).start()
                return carry

            lax.fori_loop(low, high, send, 0)

    loads[1].wait()
    loads[0].wait()
    send_own(0, FIRST)

    entry = start[0] + tm * 2
    line = lax.broadcasted_iota(jnp.int32, (8, 112), 0)
    wanted = entry + jnp.where(line == 0, zh, 1 - zh)
    pick = (lax.broadcasted_iota(jnp.int32, (8, 112), 1) == wanted).astype(F32)
    step = jnp.sum(pick[0:1] * steps[...], axis=1, keepdims=True)
    pick = pick.astype(BF16)
    loads[5].wait()
    for k in range(10):
        MODS[k] = nn(pick, TABLE[k])
    GAINS[0] = jnp.broadcast_to(q_gain[...], (128, 64)).T
    GAINS[1] = jnp.broadcast_to(k_gain[...], (128, 64)).T

    loads[2].wait()
    loads[3].wait()
    loads[4].wait()
    send_own(FIRST, CHUNKS)

    def pump_x(c):
        x_copy(c).wait_recv()
        core_copy(c).start()

    def pump(c, carry):
        @pl.when(c < CHUNKS)
        def _():
            z_copy(c).wait_recv()

            @pl.when(jnp.logical_not(first))
            def _():
                z_copy(c).start()

            x_copy(c).start()

        @pl.when(c >= LAG)
        def _():
            pump_x(c - LAG)

        return carry

    def arrive(c, carry):
        core_copy(c).wait_recv()
        return carry

    mine = pl.ds(pl.multiple_of(core * 96, 16), 96)

    def wo_copy(part, k):
        return copy(
            WB.at[part, pl.ds(pl.multiple_of(WO_AT + core * 96, 16), 96)],
            WOF.at[y, part, mine],
            wos.at[part, k],
            wor.at[part, k],
            y_peers[k],
        )

    def wo_forward(part, k):
        at = WOF.at[(y + 3 - k) % 4, part, mine]
        return copy(at, at, wfs.at[part, k], wfr.at[part, k], other_core)

    def wo_copies(part):
        return [wo_copy(part, k) for k in range(3)]

    def wo_forwards(part):
        return [wo_forward(part, k) for k in range(3)]

    loads[6].wait()
    loads[7].wait()
    text_copy = copy(CS.at[1 - zh], CRECV, txs, txr, other_half)

    def prompt(c):
        of_other = c < 6
        slot = jnp.where(of_other, 1 - zh, zh)
        part = c % 6

        @pl.when(part < 4)
        def _():
            shift, scale = (
                jnp.where(of_other, MODS[k, 1:2, :], MODS[k, 0:1, :]) for k in (6, 7)
            )
            ln_rows(CTX, TN, shift, scale, part * 32, 32)

        @pl.when(part == 4)
        def _():
            keys = head_norm_t(nt(TT[0:192, :], TN[...]), GAINS[1])
            CS[slot, 0:192, :] = keys.reshape(192, 128).astype(BF16)

        @pl.when(part == 5)
        def _():
            CS[slot, 192:384, :] = nt(TT[192:384, :], TN[...]).astype(BF16)

        @pl.when(c == 5)
        def _():
            text_copy.start()

    def only_prompt(c, carry):
        prompt(c)
        return carry

    hop = jnp.where(core == 0, zl + 1, 4 - zl)

    def by_hop(*values):
        return jnp.where(
            hop == 1,
            values[0],
            jnp.where(hop == 2, values[1], jnp.where(hop == 3, values[2], values[3])),
        )

    ready = by_hop(6, 6, 12, 12)
    before, between, middle = by_hop(18, 16, 13, 11), by_hop(18, 18, 15, 12), by_hop(22, 22, 22, 17)
    lax.fori_loop(0, ready, only_prompt, 0)
    pump(0, 0)

    ex_x.wait()
    ex_pos.wait()
    anchor = jnp.concatenate([XR[0], XR[1]], axis=1)
    XIN[0, y] = anchor.astype(BF16)

    def state_copies(r):
        return [
            copy(XIN.at[r, y], XIN.at[r, y], gs.at[r, k], gr.at[r, k], y_peers[k])
            for k in FAR_FIRST
        ]

    pos_copies = [
        copy(POS.at[y], POS.at[y], gs.at[3, k], gr.at[3, k], y_peers[k]) for k in range(3)
    ]
    for one in state_copies(0) + pos_copies:
        one.start()
    def pump_prompt(c, carry):
        pump(c, carry)

        @pl.when(ready + c - 1 < 12)
        def _():
            prompt(ready + c - 1)

        return carry

    lax.fori_loop(1, 4, pump_prompt, 0)
    for one in wo_copies(0):
        one.start()
    lax.fori_loop(4, before, pump_prompt, 0)
    loads[8].wait()
    loads[9].wait()
    loads[10].wait()
    for one in state_copies(0) + pos_copies:
        one.wait()

    own_rows = pl.ds(pl.multiple_of(y * 32, 32), 32)
    their_rows = [
        pl.ds(pl.multiple_of(((y + k + 1) % 4) * 32, 32), 32) for k in range(3)
    ]
    start_slot = jnp.logical_and(tm == 0, zh == 0)

    def mod(k):
        return MODS[k, 0:1, :]

    def one_round(r, carry):
        halves = XIN[r].astype(F32)
        X = jnp.concatenate(
            [halves[i // 2, :, 64 * (i % 2) : 64 * (i % 2) + 64] for i in range(8)], axis=0
        ).astype(BF16)
        H[...] = nn(X, PATCH[...]) + POS[...].reshape(128, 1536).astype(F32)
        ln_rows(H, N, mod(0), mod(1), 0, 128)

        @pl.when(r == 0)
        def _():
            text_copy.wait()
            for i in range(3):
                at = slice(i * 64, (i + 1) * 64)
                CKN[0, i] = CS[zh, at, :].astype(F32).T.astype(BF16)
                CKN[1, i] = CRECV[at, :].astype(F32).T.astype(BF16)
            CVT[0] = CS[zh, 192:384, :]
            CVT[1] = CRECV[192:384, :]
            lax.fori_loop(0, FIRST, arrive, 0)
            for k in (0, 2):
                wo_copy(1, k).start()

        parts = []

        def head_copies(p):
            at = pl.ds(p * 128, 128)
            return [
                copy(
                    AB.at[r, y, :, at],
                    AB.at[r, y, :, at],
                    ats.at[r, p, k],
                    atr.at[r, p, k],
                    y_peers[k],
                )
                for k in FAR_FIRST
            ]

        def send_heads(p):
            AB[r, y, :, p * 128 : (p + 1) * 128] = jnp.concatenate(parts, axis=0).T.astype(BF16)
            parts.clear()

            @pl.when(r > 0)
            def _():
                for one in head_copies(p):
                    one.start()

        attended = [head_copies(p) for p in range(3)]
        for s in range(2):
            if s == 1:

                @pl.when(r == 0)
                def _():
                    lax.fori_loop(before, between, pump, 0)

            joint = nt(WB[s, HEADS_AT:WO_AT, :], N[...])
            query = head_norm_t(joint[:192], GAINS[0]).astype(BF16)
            keys = head_norm_t(joint[192:384], GAINS[1])
            values = joint[384:].astype(BF16)
            for i in range(3):
                key_rows = jnp.concatenate([keys[i].T.astype(BF16), CKN[s, i]], axis=0)
                scores = nn(key_rows, query[i]) * 0.125
                powers = jnp.exp(scores)
                probs = (powers / jnp.sum(powers, axis=0, keepdims=True)).astype(BF16)
                both = jnp.concatenate(
                    [values[i * 64 : (i + 1) * 64], CVT[s, i * 64 : (i + 1) * 64, :]], axis=1
                )
                parts.append(nn(both, probs))
                if len(parts) == 2:
                    send_heads((3 * s + i) // 2)

        @pl.when(r == 0)
        def _():
            ACC[...] = nn(AB[r, y, :, 0:192], WB[0, WO_AT:UP_AT, :]) + nn(
                AB[r, y, :, 192:384], WB[1, WO_AT:UP_AT, :]
            )
            RSS[1] = ACC[...].astype(BF16)
            mixed = [
                copy(RSS.at[1, their_rows[k]], RSB.at[3, k], mxs.at[0, k], mxr.at[0, k], y_peers[k])
                for k in FAR_FIRST
            ]
            for one in mixed:
                one.start()
            lax.fori_loop(between, middle, pump, 0)
            for one in mixed:
                one.wait_recv()
            total = ACC[own_rows, :]
            for k in range(3):
                total = total + RSB[3, k].astype(F32)
            H[own_rows, :] = H[own_rows, :] + mod(2) * total
            ln_rows(H, N, mod(3), mod(4), y * 32, 32)
            normed = [
                copy(N.at[own_rows], N.at[own_rows], mxs.at[1, k], mxr.at[1, k], y_peers[k])
                for k in FAR_FIRST
            ]
            for one in normed:
                one.start()
            lax.fori_loop(middle, STEPS, pump, 0)
            for part, k in ((0, 0), (0, 2), (0, 1), (1, 0), (1, 2)):
                wo_copy(part, k).wait_recv()
                wo_forward(part, k).start()
            fill = pltpu.make_async_copy(
                WB.at[1, pl.ds(WO_AT, 192)], WOF.at[y, 1], local.at[11]
            )
            fill.start()
            lax.fori_loop(FIRST, CHUNKS, arrive, 0)
            fill.wait()
            for one in normed:
                one.wait_recv()
            for one in mixed + normed:
                one.wait_send()

        @pl.when(r == 1)
        def _():
            wo_copy(1, 1).wait_recv()
            wo_forward(1, 1).start()
            for part in range(2):
                for forward in wo_forwards(part):
                    forward.wait_recv()

        def project(k):
            return nn(AB[r, (y + k) % 4], WOF[(y + k) % 4].reshape(384, 1536))

        @pl.when(r > 0)
        def _():
            ACC[...] = project(0)
            for k, i in ((1, 2), (3, 1), (2, 0)):
                for p in range(3):
                    attended[p][i].wait_recv()
                ACC[...] += project(k)
            H[...] = H[...] + mod(2) * ACC[...]
            ln_rows(H, N, mod(3), mod(4), 0, 128)

        active = []
        for s in range(2):
            hidden = nn(N[:, 0:768], WB[s, UP_AT:DOWN_AT, 0:768]) + nn(
                N[:, 768:1536], WB[s, UP_AT:DOWN_AT, 768:1536]
            )
            active.append(jax.nn.gelu(hidden, approximate=True).astype(BF16))

        summed = []
        for p in range(2):
            at = slice(p * 768, (p + 1) * 768)
            total = nn(active[0], WB[0, DOWN_AT:ALL_ROWS, at]) + nn(
                active[1], WB[1, DOWN_AT:ALL_ROWS, at]
            )
            ACC[:, at] = total
            RSS[0, :, at] = total.astype(BF16)
            for k in FAR_FIRST:
                one = copy(
                    RSS.at[0, their_rows[k], pl.ds(p * 768, 768)],
                    RSB.at[r, k, :, pl.ds(p * 768, 768)],
                    rss.at[r, p, k],
                    rsr.at[r, p, k],
                    y_peers[k],
                )
                one.start()
                summed.append(one)
        for one in summed:
            one.wait_recv()

        @pl.when(r == 0)
        def _():
            wo_copy(1, 1).start()

        contract = ACC[own_rows, :]
        for k in range(3):
            contract = contract + RSB[r, k].astype(F32)
        state = ln_mod(H[own_rows, :] + mod(5) * contract, mod(8), mod(9))
        term = step * nt(state, FINAL[...])
        term = jnp.concatenate([term[0:16], term[16:32]], axis=1)
        anchor = jnp.concatenate([XR[0], XR[1]], axis=1)
        term = term - jnp.where(start_slot, anchor, jnp.zeros_like(anchor))

        TZ[r, z] = term
        along_z = [
            copy(TZ.at[r, z], TZ.at[r, z], szs.at[r, k - 1], szr.at[r, k - 1], z_peers[k - 1])
            for k in (4, 3, 5, 2, 6, 1, 7)
        ]
        for one in along_z:
            one.start()
        for one in along_z:
            one.wait_recv()
        lower = TZ[r, zl]
        both_halves = lower + TZ[r, zl + 4]
        below = jnp.zeros_like(term)
        for i in range(8):
            block = TZ[r, i]
            below = below + jnp.where(i % 4 < zl, block, jnp.zeros_like(block))
        SUMS[r, 0] = below
        SUMS[r, 1] = below + both_halves
        XS[r, x, core] = below
        along_x = []
        for k in (4, 5, 2, 3, 6, 7, 1):
            to_x, to_core = (x + k // 2) % 4, (core + k) % 2
            later = (2 * to_x + to_core > 2 * x + core).astype(jnp.int32)
            one = copy(
                SUMS.at[r, later],
                XS.at[r, x, core],
                sxs.at[r, k - 1],
                sxr.at[r, k - 1],
                device(z, to_x, to_core, y),
            )
            one.start()
            along_x.append(one)
        for one in along_x:
            one.wait_recv()
        base = jnp.zeros_like(term)
        for i in range(8):
            base = base + XS[r, i // 2, i % 2]
        upper = zh == 1

        @pl.when(r < ROUNDS - 1)
        def _():
            earlier = base + jnp.where(upper, lower, jnp.zeros_like(lower))
            XIN[r + 1, y] = jnp.where(start_slot, anchor, -earlier).astype(BF16)
            for one in state_copies(r + 1):
                one.start()
            for one in state_copies(r + 1):
                one.wait()

        @pl.when(r == ROUNDS - 1)
        def _():
            for s, total in enumerate([base + lower, base + both_halves]):
                out[s] = -jnp.where(upper, total[:, 64:128], total[:, 0:64])

        for one in summed + along_x + along_z:
            one.wait_send()

        @pl.when(r > 0)
        def _():
            for one in sum(attended, []):
                one.wait_send()

        return carry

    lax.fori_loop(0, ROUNDS, one_round, 0)

    def drain(c, carry):
        z_copy(c).wait_send()
        x_copy(c).wait_send()
        core_copy(c).wait_send()
        return carry

    lax.fori_loop(0, CHUNKS, drain, 0)
    for part in range(2):
        for one in wo_copies(part) + wo_forwards(part):
            one.wait_send()


def per_device(
    trajectory,
    window_start,
    step_sizes,
    modulation,
    context,
    position_embed,
    patch_weight,
    heads_weight,
    query_gain,
    key_gain,
    text_weight,
    output_weight,
    up_weight,
    down_weight,
    final_weight,
):
    heads = heads_weight.transpose(1, 2, 0).reshape(HEAD_ROWS, 1536)
    text = text_weight.transpose(1, 2, 0).reshape(384, 1536)
    vmem = pl.BlockSpec(memory_space=pltpu.VMEM)
    hbm = pl.BlockSpec(memory_space=pl.ANY)
    dma = pltpu.SemaphoreType.DMA
    R = ROUNDS
    return pl.pallas_call(
        kernel,
        out_shape=jax.ShapeDtypeStruct((2, 16, 64), F32),
        in_specs=[vmem, pl.BlockSpec(memory_space=pltpu.SMEM), vmem, hbm, hbm, vmem, hbm, hbm]
        + [vmem, vmem, hbm, hbm, hbm, hbm, hbm],
        out_specs=vmem,
        scratch_shapes=[
            pltpu.VMEM((2, ALL_ROWS, 1536), BF16),
            pltpu.VMEM((4, 2, 192, 1536), BF16),
            pltpu.VMEM((384, 1536), BF16),
            pltpu.VMEM((4, 32, 1536), BF16),
            pltpu.VMEM((R, 4, 16, 128), BF16),
            pltpu.VMEM((2, 16, 64), F32),
            pltpu.VMEM((128, 1536), BF16),
            pltpu.VMEM((2, 3, 128, 64), BF16),
            pltpu.VMEM((2, 192, 128), BF16),
            pltpu.VMEM((2, 384, 128), BF16),
            pltpu.VMEM((384, 128), BF16),
            pltpu.VMEM((128, 1536), F32),
            pltpu.VMEM((128, 1536), BF16),
            pltpu.VMEM((128, 1536), F32),
            pltpu.VMEM((R, 4, 128, 384), BF16),
            pltpu.VMEM((2, 128, 1536), BF16),
            pltpu.VMEM((R + 1, 3, 32, 1536), BF16),
            pltpu.VMEM((R, 8, 16, 128), F32),
            pltpu.VMEM((R, 2, 16, 128), F32),
            pltpu.VMEM((R, 4, 2, 16, 128), F32),
            pltpu.VMEM((10, 112, 1536), BF16),
            pltpu.VMEM((10, 8, 1536), F32),
            pltpu.VMEM((128, 1536), BF16),
            pltpu.VMEM((64, 1536), BF16),
            pltpu.VMEM((64, 1536), BF16),
            pltpu.VMEM((2, 64, 128), F32),
            dma((12,)),
            dma((CHUNKS,)),
            dma((CHUNKS,)),
            dma((CHUNKS,)),
            dma((CHUNKS,)),
            dma((CHUNKS,)),
            dma((CHUNKS,)),
            dma((2, 3)),
            dma((2, 3)),
            dma((2, 3)),
            dma((2, 3)),
            dma((2,)),
            dma((2,)),
            dma((4, 3)),
            dma((4, 3)),
            dma,
            dma,
            dma((R, 3, 3)),
            dma((R, 3, 3)),
            dma((R, 2, 3)),
            dma((R, 2, 3)),
            dma((R, 7)),
            dma((R, 7)),
            dma((R, 7)),
            dma((R, 7)),
            dma((2, 3)),
            dma((2, 3)),
        ],
        compiler_params=pltpu.CompilerParams(
            collective_id=0, has_side_effects=True, vmem_limit_bytes=56 << 20
        ),
        cost_estimate=pl.CostEstimate(
            flops=7_000_000_000, bytes_accessed=10_000_000, transcendentals=1_000_000
        ),
        name="picard",
    )(
        trajectory,
        window_start,
        step_sizes[None],
        modulation.transpose(1, 0, 2),
        context,
        position_embed,
        patch_weight,
        heads,
        query_gain[None],
        key_gain[None],
        text,
        output_weight,
        up_weight,
        down_weight,
        final_weight.T,
    )


def solution(mesh):
    return jax.shard_map(
        per_device,
        mesh=mesh,
        in_specs=(
            P("tm", "tp", None),
            P(),
            P(),
            P(),
            P(),
            P("tp", None),
            P(),
            P(None, None, "tp"),
            P(),
            P(),
            P(None, None, "tp"),
            P("tp", None),
            P(None, "tp"),
            P("tp", None),
            P(),
        ),
        out_specs=P("tm", "tp", None),
        check_vma=False,
    )
```
